32 devices in a mesh: grp: 2 (over y), row: 4 (over z), col: 2 (over x), pair: 2 (over core).
Axes of the slice: x: 2, y: 2, z: 4, core: 2. Of those that a mesh axis runs over, the one named last changes fastest.
Arguments:
- features_in: bfloat16 [128, 32, 512], P('grp', 'row', ('col', 'pair')), parts along dimension 0, may hold values from -8 to 8
- filters_one: bfloat16 [64, 3, 3, 64], replicated, may hold values from -0.25 to 0.25
- filters_two: bfloat16 [512, 3, 3, 256], P('row'), may hold values from -0.125 to 0.125
- out_grad: bfloat16 [1024, 128, 8], P(('grp', 'row'), ('col', 'pair')), parts along dimension 0, may hold values from -24 to 24
Outputs:
- input_grad: bfloat16 [128, 32, 512], P('grp', 'row', ('col', 'pair')), parts along dimension 0
- grad_one: float32 [128, 3, 3, 64], P('grp'), parts along dimension 0
- grad_two: float32 [1024, 3, 3, 256], P(('grp', 'row')), parts along dimension 0
The draws below stay inside these ranges and needn't reach their ends.
There are 2 independent parts, one for each index of `grp`. The reference program is written for one: setup_inputs(seed, part) draws one part's arguments, and reference() takes and returns one part's arrays. A program takes and returns all parts, laid end to end along the dimension named above; an argument that names none is the same for every part. Nothing has to cross between parts.
All inputs are finite; a program needn't handle non-finite values.
Results may differ from the reference program's by a relative error of at most 0.015.
Values may be sent and summed in bfloat16 or wider, within the bound.
A program may use at most 64 MiB of HBM per device.

```python
import math
import jax
import jax.numpy as jnp
from jax import lax

C1 = 64
F2 = 512
C2 = 256
H = 32
W = 512
H2 = 8
W2 = 128


def mixed_field(key, shape, base_scale):
    values = jax.random.normal(jax.random.fold_in(key, 13), shape, jnp.float32)
    return (jnp.clip(values, -6.0, 6.0) * base_scale).astype(jnp.bfloat16)


def draw_features_in(key, part):
    return mixed_field(key, (C1, H, W), 1.0)


def draw_out_grad(key, part):
    return mixed_field(key, (F2, W2, H2), 3.0)


def level_of(stream_key, extent, split, low, top_value):
    level, own = 1.0, jax.random.fold_in(stream_key, 6)
    for position, shards_of in split:
        heights = jnp.exp(jax.random.uniform(jax.random.fold_in(own, position), (shards_of,), jnp.float32, low / len(split), top_value / len(split)))
        level = level * jnp.repeat(heights, extent[position] // shards_of).reshape([-1 if axis == position else 1 for axis in range(len(extent))])
    return level


def noise(stream_key, shape, width, most, pieces=(), held_as=jnp.bfloat16):
    entries = jax.random.normal(stream_key, shape, jnp.float32) * width
    if len(pieces) > 0:
        entries = level_of(stream_key, shape, pieces, -0.22, 0.18) * entries
    return jnp.clip(entries, min=-most, max=most).astype(held_as)


def setup_inputs(seed: int = 0, part: int = 0) -> dict:
    splits = jax.random.split(jax.random.key(seed), 5)
    own_keys = jax.random.split(jax.random.fold_in(splits[4], part), 5)
    features_in = draw_features_in(jax.random.fold_in(jax.random.fold_in(splits[4], part), 71), part)
    filters_one = noise(splits[1], (C1, 3, 3, C1), (9 * C1) ** -0.5, 0.25)
    filters_two = noise(splits[2], (F2, 3, 3, C2), (9 * C2) ** -0.5, 0.125, ((0, 4),))
    out_grad = draw_out_grad(jax.random.fold_in(jax.random.fold_in(splits[4], part), 71), part)
    return dict(features_in=features_in, filters_one=filters_one, filters_two=filters_two, out_grad=out_grad)


def conv_same(values, kernel):
    return lax.conv_general_dilated(values.astype(jnp.float32)[None], kernel.astype(jnp.float32), (1, 1), ((1, 1), (1, 1)), dimension_numbers=('NCHW', 'OHWI', 'NCHW'), precision=lax.Precision.HIGHEST)[0]

def conv_back(gradient, kernel):
    flipped = jnp.transpose(kernel[:, ::-1, ::-1, :], (3, 1, 2, 0))
    return conv_same(gradient, flipped)

def filter_grad(gradient, values):
    padded = jnp.pad(values.astype(jnp.float32), ((0, 0), (1, 1), (1, 1)))
    row_count, col_count = (gradient.shape[1], gradient.shape[2])
    wide_grad = gradient.astype(jnp.float32)
    tap_list = []
    for row_tap in range(3):
        tap_row = []
        for col_tap in range(3):
            window = padded[:, row_tap:row_tap + row_count, col_tap:col_tap + col_count]
            tap_row.append(jnp.einsum('ohw,chw->oc', wide_grad, window, precision=lax.Precision.HIGHEST))
        tap_list.append(jnp.stack(tap_row, 1))
    return jnp.stack(tap_list, 1)

def silu_slope(values):
    sigmoid_value = jax.nn.sigmoid(values)
    return sigmoid_value * (1.0 + values * (1.0 - sigmoid_value))

def pool_map(active):
    channels, row_count, col_count = active.shape
    folded = active.reshape(channels, row_count // 4, 2, 2, col_count // 4, 2, 2).mean(axis=(3, 6))
    return jnp.transpose(folded, (0, 2, 4, 1, 3)).reshape(channels * 4, row_count // 4, col_count // 4)

def unpool_map(gradient):
    quad_count, row_count, col_count = gradient.shape
    ordered = jnp.transpose(gradient.reshape(quad_count // 4, 2, 2, row_count, col_count), (0, 3, 1, 4, 2))
    spread = jnp.broadcast_to(ordered[:, :, :, None, :, :, None], (quad_count // 4, row_count, 2, 2, col_count, 2, 2)) * 0.25
    return spread.reshape(quad_count // 4, row_count * 4, col_count * 4)

def reference(features_in, filters_one, filters_two, out_grad):
    pre_one = conv_same(features_in, filters_one)
    pooled = pool_map(jax.nn.silu(pre_one)).astype(jnp.bfloat16)
    pre_two = conv_same(pooled, filters_two)
    grad_pre_two = (jnp.transpose(out_grad, (0, 2, 1)).astype(jnp.float32) * silu_slope(pre_two)).astype(jnp.bfloat16)
    grad_two = filter_grad(grad_pre_two, pooled) / math.sqrt(H2 * W2)
    grad_pooled = conv_back(grad_pre_two, filters_two)
    grad_pre_one = (unpool_map(grad_pooled) * silu_slope(pre_one)).astype(jnp.bfloat16)
    grad_one = filter_grad(grad_pre_one, features_in) / math.sqrt(H * W)
    input_grad = conv_back(grad_pre_one, filters_one).astype(jnp.bfloat16)
    return (input_grad, grad_one, grad_two)
```

```python
import functools
import math

import jax
import jax.numpy as jnp
from jax import lax
from jax.experimental import pallas as pl
from jax.experimental.pallas import tpu as pltpu
from jax.sharding import PartitionSpec as P

MESH = pl.DeviceIdType.MESH
VMEM = pl.BlockSpec(memory_space=pltpu.VMEM)
STRIP = ("col", "pair")


def place():
    return lax.axis_index("row"), lax.axis_index(STRIP)


def device_at(row, strip):
    pairs = lax.axis_size("pair")
    return (lax.axis_index("grp"), row, lax.div(strip, pairs), lax.rem(strip, pairs))


def params(number):
    return pltpu.CompilerParams(
        collective_id=number, has_side_effects=True, vmem_limit_bytes=40 * 1024 * 1024
    )


WAYS = [(a, b) for a in (-1, 0, 1) for b in (-1, 0, 1) if (a, b) != (0, 0)]


def halo_kernel(rows, strips, edge_rows, edge_cols, got_rows, got_cols, got_diag, send_sem, recv_sem):
    row, strip = place()

    def there(way):
        a, b = row + way[0], strip + way[1]
        return (a >= 0) & (a < rows) & (b >= 0) & (b < strips)

    barrier = pltpu.get_barrier_semaphore()
    for way in WAYS:
        @pl.when(there(way))
        def _(way=way):
            pl.semaphore_signal(
                barrier, inc=1, device_id=device_at(row + way[0], strip + way[1]), device_id_type=MESH
            )

    def landing(way):
        if way[1] == 0:
            return got_rows.at[0 if way[0] < 0 else 1]
        if way[0] == 0:
            return got_cols.at[0 if way[1] < 0 else 1]
        return got_diag.at[(0 if way[0] < 0 else 2) + (0 if way[1] < 0 else 1)]

    for way in WAYS:
        @pl.when(jnp.logical_not(there(way)))
        def _(way=way):
            slot = landing(way)
            slot[...] = jnp.zeros(slot.shape, slot.dtype)

    high = 1 + jnp.where(row > 0, 1, 0) + jnp.where(row < rows - 1, 1, 0)
    across = 1 + jnp.where(strip > 0, 1, 0) + jnp.where(strip < strips - 1, 1, 0)
    pl.semaphore_wait(barrier, high * across - 1)

    def copy_to(way):
        back = (-way[0], -way[1])
        if way[1] == 0:
            source = edge_rows.at[0 if way[0] < 0 else 1]
        else:
            source = edge_cols.at[0 if way[1] < 0 else 1]
        return pltpu.make_async_remote_copy(
            src_ref=source,
            dst_ref=landing(back),
            send_sem=send_sem.at[WAYS.index(way)],
            recv_sem=recv_sem.at[WAYS.index(back)],
            device_id=device_at(row + way[0], strip + way[1]),
            device_id_type=MESH,
        )

    for way in WAYS:
        @pl.when(there(way))
        def _(way=way):
            copy_to(way).start()
    for way in WAYS:
        @pl.when(there(way))
        def _(way=way):
            back = (-way[0], -way[1])
            copy_to(way).wait_send()
            copy_to(back).wait_recv()


def halo_exchange(cells, wide, number):
    channels, height, width = cells.shape
    edge_rows = jnp.stack(
        [cells[:, :wide].reshape(channels * wide, width), cells[:, -wide:].reshape(channels * wide, width)]
    )
    flat = jnp.stack(
        [cells[:, :, :wide].reshape(channels, height * wide), cells[:, :, -wide:].reshape(channels, height * wide)]
    )
    edge_cols = jnp.pad(flat, ((0, 0), (0, 0), (0, 128 - height * wide)))
    rows, strips = lax.axis_size("row"), lax.axis_size(STRIP)
    got_rows, got_cols, got_diag = pl.pallas_call(
        functools.partial(halo_kernel, rows, strips),
        out_shape=(
            jax.ShapeDtypeStruct(edge_rows.shape, cells.dtype),
            jax.ShapeDtypeStruct(edge_cols.shape, cells.dtype),
            jax.ShapeDtypeStruct((4,) + edge_cols.shape[1:], cells.dtype),
        ),
        in_specs=[VMEM] * 2,
        out_specs=(VMEM,) * 3,
        scratch_shapes=[pltpu.SemaphoreType.DMA((8,)), pltpu.SemaphoreType.DMA((8,))],
        compiler_params=params(number),
    )(edge_rows, edge_cols)
    got_rows = got_rows.reshape(2, channels, wide, width)
    side = got_cols[:, :, : height * wide].reshape(2, channels, height, wide)
    corner = got_diag[:, :, : height * wide].reshape(4, channels, height, wide)
    above = jnp.concatenate([corner[0, :, -wide:], got_rows[0], corner[1, :, -wide:]], 2)
    middle = jnp.concatenate([side[0], cells, side[1]], 2)
    below = jnp.concatenate([corner[2, :, :wide], got_rows[1], corner[3, :, :wide]], 2)
    return jnp.concatenate([above, middle, below], 1)


def greet(count, me, device_of):
    barrier = pltpu.get_barrier_semaphore()

    @pl.loop(1, count)
    def _(step):
        pl.semaphore_signal(
            barrier, inc=1, device_id=device_of(lax.rem(me + step, count)), device_id_type=MESH
        )

    pl.semaphore_wait(barrier, count - 1)


def post(count, me, device_of, source, landing, send_sem, recv_sem):
    def copy_of(step):
        peer = lax.rem(me + step, count)
        return pltpu.make_async_remote_copy(
            src_ref=source(peer),
            dst_ref=landing.at[me],
            send_sem=send_sem.at[step],
            recv_sem=recv_sem.at[me],
            device_id=device_of(peer),
            device_id_type=MESH,
        )

    def arrival(step):
        peer = lax.rem(me + step, count)
        return pltpu.make_async_remote_copy(
            src_ref=source(peer),
            dst_ref=landing.at[peer],
            send_sem=send_sem.at[step],
            recv_sem=recv_sem.at[peer],
            device_id=device_of(peer),
            device_id_type=MESH,
        )

    @pl.loop(1, count)
    def _(step):
        copy_of(step).start()

    def finish():
        @pl.loop(1, count)
        def _(step):
            copy_of(step).wait_send()
            arrival(step).wait_recv()

    return finish


def group(kind):
    rows, strips = lax.axis_size("row"), lax.axis_size(STRIP)
    row, strip = place()
    if kind == "all":
        return (
            rows * strips,
            row * strips + strip,
            lambda i: device_at(lax.div(i, strips), lax.rem(i, strips)),
        )
    if kind == "strips":
        return strips, strip, lambda i: device_at(row, i)
    return rows, row, lambda i: device_at(i, strip)


def gather_kernel(kind, block, out, send_sem, recv_sem):
    count, me, device_of = group(kind)
    greet(count, me, device_of)
    finish = post(count, me, device_of, lambda peer: block, out, send_sem, recv_sem)
    out[me] = block[...]
    finish()


def sems(count):
    return [pltpu.SemaphoreType.DMA((count,)), pltpu.SemaphoreType.DMA((count,))]


def group_size(kind):
    rows, strips = lax.axis_size("row"), lax.axis_size(STRIP)
    return dict(all=rows * strips, strips=strips, rows=rows)[kind]


def gather(block, kind, number):
    count = group_size(kind)
    return pl.pallas_call(
        functools.partial(gather_kernel, kind),
        out_shape=jax.ShapeDtypeStruct((count,) + block.shape, block.dtype),
        in_specs=[VMEM],
        out_specs=VMEM,
        scratch_shapes=sems(count),
        compiler_params=params(number),
    )(block)


def total_of(count, landing):
    return lax.fori_loop(
        1,
        count,
        lambda i, value: value + landing[i].astype(jnp.float32),
        landing[0].astype(jnp.float32),
    )


def scatter_kernel(kind, blocks, out, landing, send_sem, recv_sem):
    count, me, device_of = group(kind)
    greet(count, me, device_of)
    finish = post(count, me, device_of, lambda peer: blocks.at[peer], landing, send_sem, recv_sem)
    landing[me] = blocks[me]
    finish()
    out[...] = total_of(count, landing)


def reduce_scatter(blocks, kind, number):
    count = group_size(kind)
    return pl.pallas_call(
        functools.partial(scatter_kernel, kind),
        out_shape=jax.ShapeDtypeStruct(blocks.shape[1:], jnp.float32),
        in_specs=[VMEM],
        out_specs=VMEM,
        scratch_shapes=[pltpu.VMEM(blocks.shape, blocks.dtype)] + sems(count),
        compiler_params=params(number),
    )(blocks)


def all_reduce_kernel(kind, blocks, out, landing, mine, send_sem, recv_sem, send_two, recv_two):
    count, me, device_of = group(kind)
    greet(count, me, device_of)
    finish = post(count, me, device_of, lambda peer: blocks.at[peer], landing, send_sem, recv_sem)
    landing[me] = blocks[me]
    finish()
    total = total_of(count, landing).astype(mine.dtype)
    mine[...] = total
    finish = post(count, me, device_of, lambda peer: mine, out, send_two, recv_two)
    out[me] = total
    finish()


def all_reduce(blocks, kind, number):
    count = group_size(kind)
    return pl.pallas_call(
        functools.partial(all_reduce_kernel, kind),
        out_shape=jax.ShapeDtypeStruct(blocks.shape, blocks.dtype),
        in_specs=[VMEM],
        out_specs=VMEM,
        scratch_shapes=[pltpu.VMEM(blocks.shape, blocks.dtype), pltpu.VMEM(blocks.shape[1:], blocks.dtype)]
        + sems(count)
        + sems(count),
        compiler_params=params(number),
    )(blocks)


def conv_valid(cells, kernel, numbers):
    return lax.conv_general_dilated(
        cells[None], kernel, (1, 1), "VALID", dimension_numbers=numbers, preferred_element_type=jnp.float32
    )[0]


def flip_kernel(kernel):
    return jnp.transpose(kernel[:, ::-1, ::-1, :], (3, 1, 2, 0))


def silu_slope(values):
    sigmoid_value = jax.nn.sigmoid(values)
    return sigmoid_value * (1.0 + values * (1.0 - sigmoid_value))


def tap_grads(gradient, padded, letters):
    row_count, col_count = gradient.shape[:2]
    taps = []
    for first in range(3):
        for second in range(3):
            if letters == "chw":
                window = padded[:, first : first + row_count, second : second + col_count]
            else:
                window = padded[first : first + row_count, second : second + col_count]
            taps.append(
                jnp.einsum("hwo," + letters + "->oc", gradient, window, preferred_element_type=jnp.float32)
            )
    return jnp.stack(taps, 1)


def local(features_in, filters_one, filters_two, out_grad):
    channels, band, width = features_in.shape
    rows, strips = lax.axis_size("row"), lax.axis_size(STRIP)
    row, strip = place()
    quads = channels * 4
    band2, width2 = band // 4, width // 4
    height2, full2 = band2 * rows, width2 * strips
    filters = filters_two.shape[0]

    features = halo_exchange(features_in, 2, 0)
    pre_one = conv_valid(features, filters_one, ("NCHW", "OHWI", "NHWC"))
    active = jax.nn.silu(pre_one[1:-1, 1:-1])
    pooled = active.reshape(band2, 2, 2, width2, 2, 2, channels).mean(axis=(2, 5))
    pooled = jnp.transpose(pooled, (0, 2, 4, 1, 3)).astype(jnp.bfloat16)
    pooled = pooled.reshape(band2 * width2, quads)

    gathered = gather(pooled, "all", 1).reshape(rows, strips, band2, width2, quads)
    whole = jnp.transpose(gathered, (0, 2, 1, 3, 4)).reshape(height2, full2, quads)
    whole = jnp.pad(whole, ((1, 1), (1, 1), (0, 0)))
    own = lax.dynamic_slice_in_dim(whole, strip * width2, width2 + 2, 1)
    pre_two = conv_valid(own, filters_two, ("NHWC", "OHWI", "NHWC"))
    upstream = jnp.transpose(out_grad, (2, 1, 0)).astype(jnp.float32)
    grad_two_own = (upstream * silu_slope(pre_two)).astype(jnp.bfloat16)

    strips_got = gather(grad_two_own.reshape(height2 * width2, filters), "strips", 2)
    grad_pre_two = jnp.transpose(
        strips_got.reshape(strips, height2, width2, filters), (1, 0, 2, 3)
    ).reshape(height2, full2, filters)

    near = lax.dynamic_slice_in_dim(
        jnp.pad(grad_pre_two, ((1, 1), (2, 2), (0, 0))), strip * width2, width2 + 4, 1
    )
    spread = conv_valid(near, flip_kernel(filters_two), ("NHWC", "OHWI", "NHWC"))
    channel = jnp.arange(quads)
    low_row = (channel // 2) % 2 == 1
    low_col = channel % 2 == 1
    tall = jnp.pad(spread, ((1, 1), (0, 0), (0, 0)))
    bands = spread.reshape(rows, band2, width2 + 2, quads)
    rim = jnp.where(
        low_row, tall[0 : height2 : band2], tall[band2 + 1 : height2 + 2 : band2]
    )
    bands = jnp.concatenate([bands, rim[:, None]], 1)
    edge = jnp.where(low_col, bands[:, :, :1], bands[:, :, -1:])
    bands = jnp.concatenate([bands[:, :, 1:-1], edge], 2).astype(jnp.bfloat16)
    spots = (band2 + 1) * (width2 + 1)
    room = -(-spots // 16) * 16
    bands = jnp.pad(bands.reshape(rows, spots, quads), ((0, 0), (0, room - spots), (0, 0)))
    grad_pooled = reduce_scatter(bands, "rows", 3)[:spots]

    grad_two = tap_grads(grad_pre_two, whole, "hwc") * (1.0 / math.sqrt(height2 * full2))
    grad_two = grad_two.reshape(filters, 3, 3, quads)

    halves = jnp.transpose(
        grad_pooled.reshape(band2 + 1, width2 + 1, channels, 2, 2), (0, 3, 1, 4, 2)
    ).reshape(2 * band2 + 2, 2 * width2 + 2, channels)
    halves = jnp.roll(halves, (1, 1), (0, 1))
    wide = jnp.repeat(jnp.repeat(halves, 2, 0), 2, 1)[1:-1, 1:-1] * 0.25
    at_row = row * band - 1 + jnp.arange(band + 2)
    at_col = strip * width - 1 + jnp.arange(width + 2)
    inside = ((at_row >= 0) & (at_row < band * rows))[:, None] & (
        (at_col >= 0) & (at_col < width * strips)
    )[None]
    grad_ext = jnp.where(inside[:, :, None], wide * silu_slope(pre_one), 0.0).astype(jnp.bfloat16)

    local_one = tap_grads(grad_ext[1:-1, 1:-1], features[:, 1:-1, 1:-1], "chw")
    local_one = local_one * (1.0 / math.sqrt(band * rows * width * strips))
    count = rows * strips
    cells = channels * 9 * channels
    piece = -(-cells // (count * 128 * 16)) * 16
    flat = jnp.pad(local_one.reshape(-1).astype(jnp.bfloat16), (0, count * piece * 128 - cells))
    summed = all_reduce(flat.reshape(count, piece, 128), "all", 4)
    grad_one = summed.reshape(-1)[:cells].reshape(channels, 3, 3, channels).astype(jnp.float32)

    input_grad = conv_valid(grad_ext, flip_kernel(filters_one), ("NHWC", "OHWI", "NCHW")).astype(jnp.bfloat16)
    return (input_grad, grad_one, grad_two)


def solution(mesh):
    in_specs = (
        P("grp", "row", ("col", "pair")),
        P(),
        P("row", None, None, None),
        P(("grp", "row"), ("col", "pair"), None),
    )
    out_specs = (
        P("grp", "row", ("col", "pair")),
        P("grp", None, None, None),
        P(("grp", "row"), None, None, None),
    )
    return jax.shard_map(local, mesh=mesh, in_specs=in_specs, out_specs=out_specs, check_vma=False)
```

```python
import functools
import math

import jax
import jax.numpy as jnp
from jax import lax
from jax.experimental import pallas as pl
from jax.experimental.pallas import tpu as pltpu
from jax.sharding import PartitionSpec as P

MESH = pl.DeviceIdType.MESH
VMEM = pl.BlockSpec(memory_space=pltpu.VMEM)
STRIP = ("col", "pair")


def place():
    return lax.axis_index("row"), lax.axis_index(STRIP)


def device_at(row, strip):
    pairs = lax.axis_size("pair")
    return (lax.axis_index("grp"), row, lax.div(strip, pairs), lax.rem(strip, pairs))


def params(number):
    return pltpu.CompilerParams(
        collective_id=number, has_side_effects=True, vmem_limit_bytes=40 * 1024 * 1024
    )


WAYS = [(a, b) for a in (-1, 0, 1) for b in (-1, 0, 1) if (a, b) != (0, 0)]


def halo_kernel(
    rows, strips, edge_rows, edge_cols, edge_up, got_rows, got_cols, got_diag, got_up, send_sem, recv_sem
):
    row, strip = place()

    def there(way):
        a, b = row + way[0], strip + way[1]
        return (a >= 0) & (a < rows) & (b >= 0) & (b < strips)

    barrier = pltpu.get_barrier_semaphore()
    for way in WAYS:
        @pl.when(there(way))
        def _(way=way):
            pl.semaphore_signal(
                barrier, inc=1, device_id=device_at(row + way[0], strip + way[1]), device_id_type=MESH
            )

    def landing(way):
        if way[1] == 0:
            return got_rows.at[0 if way[0] < 0 else 1]
        if way[0] == 0:
            return got_cols.at[0 if way[1] < 0 else 1]
        return got_diag.at[(0 if way[0] < 0 else 2) + (0 if way[1] < 0 else 1)]

    for way in WAYS:
        @pl.when(jnp.logical_not(there(way)))
        def _(way=way):
            slot = landing(way)
            slot[...] = jnp.zeros(slot.shape, slot.dtype)
            if way[0] == 0:
                slot = got_up.at[0 if way[1] < 0 else 1]
                slot[...] = jnp.zeros(slot.shape, slot.dtype)

    high = 1 + jnp.where(row > 0, 1, 0) + jnp.where(row < rows - 1, 1, 0)
    across = 1 + jnp.where(strip > 0, 1, 0) + jnp.where(strip < strips - 1, 1, 0)
    pl.semaphore_wait(barrier, high * across - 1)

    def copy_to(way):
        back = (-way[0], -way[1])
        if way[1] == 0:
            source = edge_rows.at[0 if way[0] < 0 else 1]
        else:
            source = edge_cols.at[0 if way[1] < 0 else 1]
        return pltpu.make_async_remote_copy(
            src_ref=source,
            dst_ref=landing(back),
            send_sem=send_sem.at[WAYS.index(way)],
            recv_sem=recv_sem.at[WAYS.index(back)],
            device_id=device_at(row + way[0], strip + way[1]),
            device_id_type=MESH,
        )

    def upstream_to(way):
        side = 0 if way[1] < 0 else 1
        return pltpu.make_async_remote_copy(
            src_ref=edge_up.at[side],
            dst_ref=got_up.at[1 - side],
            send_sem=send_sem.at[8 + side],
            recv_sem=recv_sem.at[9 - side],
            device_id=device_at(row, strip + way[1]),
            device_id_type=MESH,
        )

    for way in WAYS:
        @pl.when(there(way))
        def _(way=way):
            copy_to(way).start()
            if way[0] == 0:
                upstream_to(way).start()
    for way in WAYS:
        @pl.when(there(way))
        def _(way=way):
            back = (-way[0], -way[1])
            copy_to(way).wait_send()
            copy_to(back).wait_recv()
            if way[0] == 0:
                upstream_to(way).wait_send()
                upstream_to(back).wait_recv()


def pad_lanes(cells):
    return jnp.pad(cells, [(0, 0)] * (cells.ndim - 1) + [(0, -cells.shape[-1] % 128)])


def halo_exchange(cells, upstream, tall, wide, number):
    channels, height, width = cells.shape
    filters, count, height2 = upstream.shape
    edge_rows = jnp.stack(
        [cells[:, :tall].reshape(channels * tall, width), cells[:, -tall:].reshape(channels * tall, width)]
    )
    edge_cols = pad_lanes(
        jnp.stack(
            [cells[:, :, :wide].reshape(channels, height * wide), cells[:, :, -wide:].reshape(channels, height * wide)]
        )
    )
    edge_up = pad_lanes(
        jnp.stack(
            [upstream[:, :2].reshape(filters, 2 * height2), upstream[:, -2:].reshape(filters, 2 * height2)]
        )
    )
    rows, strips = lax.axis_size("row"), lax.axis_size(STRIP)
    got_rows, got_cols, got_diag, got_up = pl.pallas_call(
        functools.partial(halo_kernel, rows, strips),
        out_shape=(
            jax.ShapeDtypeStruct(edge_rows.shape, cells.dtype),
            jax.ShapeDtypeStruct(edge_cols.shape, cells.dtype),
            jax.ShapeDtypeStruct((4,) + edge_cols.shape[1:], cells.dtype),
            jax.ShapeDtypeStruct(edge_up.shape, cells.dtype),
        ),
        in_specs=[VMEM] * 3,
        out_specs=(VMEM,) * 4,
        scratch_shapes=[pltpu.SemaphoreType.DMA((10,)), pltpu.SemaphoreType.DMA((10,))],
        compiler_params=params(number),
    )(edge_rows, edge_cols, edge_up)
    got_rows = got_rows.reshape(2, channels, tall, width)
    side = got_cols[:, :, : height * wide].reshape(2, channels, height, wide)
    corner = got_diag[:, :, : height * wide].reshape(4, channels, height, wide)
    above = jnp.concatenate([corner[0, :, -tall:], got_rows[0], corner[1, :, -tall:]], 2)
    middle = jnp.concatenate([side[0], cells, side[1]], 2)
    below = jnp.concatenate([corner[2, :, :tall], got_rows[1], corner[3, :, :tall]], 2)
    got_up = got_up[:, :, : 2 * height2].reshape(2, filters, 2, height2)
    return (
        jnp.concatenate([above, middle, below], 1),
        jnp.concatenate([got_up[0], upstream, got_up[1]], 1),
    )


def greet(count, me, device_of):
    barrier = pltpu.get_barrier_semaphore()

    @pl.loop(1, count)
    def _(step):
        pl.semaphore_signal(
            barrier, inc=1, device_id=device_of(lax.rem(me + step, count)), device_id_type=MESH
        )

    pl.semaphore_wait(barrier, count - 1)


def post(count, me, device_of, source, landing, send_sem, recv_sem):
    def copy_of(step):
        peer = lax.rem(me + step, count)
        return pltpu.make_async_remote_copy(
            src_ref=source(peer),
            dst_ref=landing.at[me],
            send_sem=send_sem.at[step],
            recv_sem=recv_sem.at[me],
            device_id=device_of(peer),
            device_id_type=MESH,
        )

    def arrival(step):
        peer = lax.rem(me + step, count)
        return pltpu.make_async_remote_copy(
            src_ref=source(peer),
            dst_ref=landing.at[peer],
            send_sem=send_sem.at[step],
            recv_sem=recv_sem.at[peer],
            device_id=device_of(peer),
            device_id_type=MESH,
        )

    @pl.loop(1, count)
    def _(step):
        copy_of(step).start()

    def finish():
        @pl.loop(1, count)
        def _(step):
            copy_of(step).wait_send()
            arrival(step).wait_recv()

    return finish


def group(kind):
    rows, strips = lax.axis_size("row"), lax.axis_size(STRIP)
    row, strip = place()
    if kind == "all":
        return (
            rows * strips,
            row * strips + strip,
            lambda i: device_at(lax.div(i, strips), lax.rem(i, strips)),
        )
    if kind == "strips":
        return strips, strip, lambda i: device_at(row, i)
    return rows, row, lambda i: device_at(i, strip)


def gather_kernel(kind, block, out, send_sem, recv_sem):
    count, me, device_of = group(kind)
    greet(count, me, device_of)
    finish = post(count, me, device_of, lambda peer: block, out, send_sem, recv_sem)
    out[me] = block[...]
    finish()


def sems(count):
    return [pltpu.SemaphoreType.DMA((count,)), pltpu.SemaphoreType.DMA((count,))]


def group_size(kind):
    rows, strips = lax.axis_size("row"), lax.axis_size(STRIP)
    return dict(all=rows * strips, strips=strips, rows=rows)[kind]


def gather(block, kind, number):
    count = group_size(kind)
    return pl.pallas_call(
        functools.partial(gather_kernel, kind),
        out_shape=jax.ShapeDtypeStruct((count,) + block.shape, block.dtype),
        in_specs=[VMEM],
        out_specs=VMEM,
        scratch_shapes=sems(count),
        compiler_params=params(number),
    )(block)


def total_of(count, landing):
    return lax.fori_loop(
        1,
        count,
        lambda i, value: value + landing[i].astype(jnp.float32),
        landing[0].astype(jnp.float32),
    )


def scatter_kernel(
    blocks, strip_map, out, maps, landing, send_sem, recv_sem, map_send, map_recv, on_send
):
    rows, me, row_device = group("rows")
    row, strip = place()
    cols, pairs = lax.axis_size("col"), lax.axis_size("pair")
    col, pair = lax.axis_index("col"), lax.axis_index("pair")

    barrier = pltpu.get_barrier_semaphore()
    for step in range(1, rows):
        pl.semaphore_signal(
            barrier, inc=1, device_id=row_device(lax.rem(me + step, rows)), device_id_type=MESH
        )
    for step in range(1, cols):
        pl.semaphore_signal(
            barrier,
            inc=1,
            device_id=device_at(row, lax.rem(col + step, cols) * pairs + pair),
            device_id_type=MESH,
        )
    for step in range(1, pairs):
        pl.semaphore_signal(
            barrier,
            inc=1,
            device_id=device_at(row, col * pairs + lax.rem(pair + step, pairs)),
            device_id_type=MESH,
        )
    pl.semaphore_wait(barrier, rows + cols + pairs - 3)

    def across(step):
        return pltpu.make_async_remote_copy(
            src_ref=strip_map,
            dst_ref=maps.at[strip],
            send_sem=map_send.at[step],
            recv_sem=map_recv.at[strip],
            device_id=device_at(row, lax.rem(col + step, cols) * pairs + pair),
            device_id_type=MESH,
        )

    def onward(source, column, step):
        slot = column * pairs + pair
        return pltpu.make_async_remote_copy(
            src_ref=source,
            dst_ref=maps.at[slot],
            send_sem=on_send.at[column * pairs + step],
            recv_sem=map_recv.at[slot],
            device_id=device_at(row, col * pairs + lax.rem(pair + step, pairs)),
            device_id_type=MESH,
        )

    def arrival(slot):
        return pltpu.make_async_remote_copy(
            src_ref=strip_map,
            dst_ref=maps.at[slot],
            send_sem=map_send.at[0],
            recv_sem=map_recv.at[slot],
            device_id=device_at(row, strip),
            device_id_type=MESH,
        )

    for step in range(1, cols):
        across(step).start()
    finish = post(rows, me, row_device, lambda peer: blocks.at[peer], landing, send_sem, recv_sem)
    for step in range(1, pairs):
        onward(strip_map, col, step).start()
    landing[me] = blocks[me]
    maps[strip] = strip_map[...]
    for step in range(1, cols):
        column = lax.rem(col + step, cols)
        slot = column * pairs + pair
        arrival(slot).wait_recv()
        for other in range(1, pairs):
            onward(maps.at[slot], column, other).start()
    finish()
    out[...] = total_of(rows, landing).astype(out.dtype)
    for step in range(1, cols):
        across(step).wait_send()
    for step in range(cols):
        column = lax.rem(col + step, cols)
        for other in range(1, pairs):
            onward(strip_map, column, other).wait_send()
            arrival(column * pairs + lax.rem(pair + other, pairs)).wait_recv()


def reduce_scatter(blocks, strip_map, number):
    rows, strips = group_size("rows"), group_size("strips")
    return pl.pallas_call(
        scatter_kernel,
        out_shape=(
            jax.ShapeDtypeStruct(blocks.shape[1:], jnp.bfloat16),
            jax.ShapeDtypeStruct((strips,) + strip_map.shape, strip_map.dtype),
        ),
        in_specs=[VMEM] * 2,
        out_specs=(VMEM,) * 2,
        scratch_shapes=[pltpu.VMEM(blocks.shape, blocks.dtype)]
        + sems(rows)
        + sems(strips)
        + [pltpu.SemaphoreType.DMA((strips,))],
        compiler_params=params(number),
    )(blocks, strip_map)


def all_reduce_kernel(blocks, out, landing, part, parts, mine, *semaphores):
    rows, row, row_device = group("rows")
    strips, strip, strip_device = group("strips")
    barrier = pltpu.get_barrier_semaphore()
    for step in range(1, rows):
        pl.semaphore_signal(
            barrier, inc=1, device_id=row_device(lax.rem(row + step, rows)), device_id_type=MESH
        )
    for step in range(1, strips):
        pl.semaphore_signal(
            barrier, inc=1, device_id=strip_device(lax.rem(strip + step, strips)), device_id_type=MESH
        )
    pl.semaphore_wait(barrier, rows + strips - 2)
    one, two, three = semaphores[:2], semaphores[2:4], semaphores[4:]
    finish = post(strips, strip, strip_device, lambda peer: blocks.at[peer], landing, *one)
    landing[strip] = blocks[strip]
    finish()
    total = total_of(strips, landing).astype(part.dtype)
    part[...] = total
    finish = post(rows, row, row_device, lambda peer: part, parts, *two)
    parts[row] = total
    finish()
    total = total_of(rows, parts).astype(part.dtype)
    mine[...] = total
    finish = post(strips, strip, strip_device, lambda peer: mine, out, *three)
    out[strip] = total
    finish()


def all_reduce(blocks, number):
    rows, strips = group_size("rows"), group_size("strips")
    piece, kind = blocks.shape[1:], blocks.dtype
    return pl.pallas_call(
        all_reduce_kernel,
        out_shape=jax.ShapeDtypeStruct(blocks.shape, kind),
        in_specs=[VMEM],
        out_specs=VMEM,
        scratch_shapes=[
            pltpu.VMEM(blocks.shape, kind),
            pltpu.VMEM(piece, kind),
            pltpu.VMEM((rows,) + piece, kind),
            pltpu.VMEM(piece, kind),
        ]
        + sems(strips)
        + sems(rows)
        + sems(strips),
        compiler_params=params(number),
    )(blocks)


def conv_valid(cells, kernel, numbers):
    return lax.conv_general_dilated(
        cells[None], kernel, (1, 1), "VALID", dimension_numbers=numbers, preferred_element_type=jnp.float32
    )[0]


def flip_kernel(kernel):
    return jnp.transpose(kernel[:, ::-1, ::-1, :], (3, 1, 2, 0))


def silu_slope(values):
    sigmoid_value = jax.nn.sigmoid(values)
    return sigmoid_value * (1.0 + values * (1.0 - sigmoid_value))


def tap_grads(gradient, padded, scale, letters, spatial):
    row_count, col_count = (gradient.shape[axis] for axis in spatial)
    taps = []
    for first in range(3):
        for second in range(3):
            window = lax.slice_in_dim(padded, first, first + row_count, axis=spatial[0])
            window = lax.slice_in_dim(window, second, second + col_count, axis=spatial[1])
            taps.append(
                jnp.einsum(letters, gradient, window, preferred_element_type=jnp.float32) * scale
            )
    return jnp.stack(taps, 1)


def local(features_in, filters_one, filters_two, out_grad):
    channels, band, width = features_in.shape
    rows, strips = lax.axis_size("row"), lax.axis_size(STRIP)
    row, strip = place()
    quads = channels * 4
    band2, width2 = band // 4, width // 4
    height2, full2 = band2 * rows, width2 * strips
    filters = filters_two.shape[0]

    features, upstream = halo_exchange(features_in, out_grad, 2, 13, 0)
    pre_one = conv_valid(features, filters_one, ("NCHW", "OHWI", "NCHW"))
    active = jax.nn.silu(pre_one[:, 1:-1])
    near2 = width2 + 6
    pooled = active.reshape(channels, band2, 2, 2, near2, 2, 2).mean(axis=(3, 6))
    at_col = strip * width2 - 3 + jnp.arange(near2)
    inside = ((at_col >= 0) & (at_col < full2))[None, :, None]
    pooled = jnp.transpose(pooled, (1, 3, 0, 2, 4)).reshape(band2, near2, quads)
    pooled = jnp.where(inside, pooled, 0.0).astype(jnp.bfloat16).reshape(band2 * near2, quads)
    spots = band2 * near2
    pooled = jnp.pad(pooled, ((0, -spots % 16), (0, 0)))

    own = gather(pooled, "rows", 1)[:, :spots].reshape(height2, near2, quads)
    pre_two = conv_valid(
        jnp.pad(own, ((1, 1), (0, 0), (0, 0))), filters_two, ("NHWC", "OHWI", "NHWC")
    )
    upstream = jnp.transpose(upstream, (2, 1, 0)).astype(jnp.float32)
    near = (upstream * silu_slope(pre_two)).astype(jnp.bfloat16)

    spread = conv_valid(
        jnp.pad(near, ((1, 1), (0, 0), (0, 0))), flip_kernel(filters_two), ("NHWC", "OHWI", "NHWC")
    )
    channel = jnp.arange(quads)
    low_row = (channel // 2) % 2 == 1
    low_col = channel % 2 == 1
    tall = jnp.pad(spread, ((1, 1), (0, 0), (0, 0)))
    bands = spread.reshape(rows, band2, width2 + 2, quads)
    rim = jnp.where(low_row, tall[0:height2:band2], tall[band2 + 1 : height2 + 2 : band2])
    bands = jnp.concatenate([bands, rim[:, None]], 1)
    edge = jnp.where(low_col, bands[:, :, :1], bands[:, :, -1:])
    bands = jnp.concatenate([bands[:, :, 1:-1], edge], 2).astype(jnp.bfloat16)
    spots = (band2 + 1) * (width2 + 1)
    bands = jnp.pad(bands.reshape(rows, spots, quads), ((0, 0), (0, -spots % 16), (0, 0)))
    strip_map = jnp.concatenate([own[:, 3:-3], near[:, 2:-2]], 2).reshape(height2 * width2, quads + filters)
    grad_pooled, maps = reduce_scatter(bands, strip_map, 2)

    by_part = jnp.arange(quads)
    order = 4 * (by_part % channels) + by_part // channels
    pick = (channel[:, None] == order[None]).astype(jnp.bfloat16)
    parts = jnp.dot(grad_pooled[:spots], pick, preferred_element_type=jnp.float32).astype(jnp.bfloat16)
    parts = parts.reshape(band2 + 1, width2 + 1, 2, 2, channels)
    source = (jnp.arange(width + 2) + 1) // 2
    source = jnp.where(source == 0, 2 * width2 + 1, source - 1)
    place_of = 2 * jnp.arange(width2 + 1)[:, None] + jnp.arange(2)[None]
    expand = (place_of[:, :, None] == source[None, None]).astype(jnp.bfloat16)
    halves = jnp.einsum("uvijc,vjw->uicw", parts, expand, preferred_element_type=jnp.float32)
    halves = halves.reshape(2 * band2 + 2, channels, width + 2)
    halves = jnp.concatenate([halves[-1:], halves[:-1]], 0)
    tall_grad = jnp.repeat(halves, 2, 0)[1:-1] * 0.25
    at_row = row * band - 1 + jnp.arange(band + 2)
    at_col = strip * width - 1 + jnp.arange(width + 2)
    inside = ((at_row >= 0) & (at_row < band * rows))[:, None, None] & (
        (at_col >= 0) & (at_col < width * strips)
    )
    slope = jnp.transpose(silu_slope(pre_one[:, :, 11:-11]), (1, 0, 2))
    grad_ext = jnp.where(inside, tall_grad * slope, 0.0).astype(jnp.bfloat16)

    cells = channels * 9 * channels
    near_in = jnp.transpose(features[:, 1:-1, 12:-12], (1, 0, 2))
    scale = 1.0 / math.sqrt(band * rows * width * strips)
    local_one = tap_grads(grad_ext[1:-1, :, 1:-1], near_in, scale, "how,hcw->oc", (0, 2))
    piece = -(-cells // (strips * 128 * 16)) * 16
    flat = jnp.pad(local_one.reshape(-1).astype(jnp.bfloat16), (0, strips * piece * 128 - cells))
    summed = all_reduce(flat.reshape(strips, piece, 128), 3)
    grad_one = summed.reshape(-1)[:cells].reshape(channels, 3, 3, channels).astype(jnp.float32)

    input_grad = conv_valid(
        jnp.transpose(grad_ext, (1, 0, 2)), flip_kernel(filters_one), ("NCHW", "OHWI", "NCHW")
    ).astype(jnp.bfloat16)

    maps = jnp.transpose(maps.reshape(strips, height2, width2, quads + filters), (1, 0, 2, 3))
    maps = maps.reshape(height2, full2, quads + filters)
    whole = jnp.pad(maps[:, :, :quads], ((1, 1), (1, 1), (0, 0)))
    grad_two = tap_grads(
        maps[:, :, quads:], whole, 1.0 / math.sqrt(height2 * full2), "hwo,hwc->oc", (0, 1)
    )
    return (input_grad, grad_one, grad_two.reshape(filters, 3, 3, quads))


def solution(mesh):
    in_specs = (
        P("grp", "row", ("col", "pair")),
        P(),
        P("row", None, None, None),
        P(("grp", "row"), ("col", "pair"), None),
    )
    out_specs = (
        P("grp", "row", ("col", "pair")),
        P("grp", None, None, None),
        P(("grp", "row"), None, None, None),
    )
    return jax.shard_map(local, mesh=mesh, in_specs=in_specs, out_specs=out_specs, check_vma=False)
```

```python
import functools
import math

import jax
import jax.numpy as jnp
from jax import lax
from jax.experimental import pallas as pl
from jax.experimental.pallas import tpu as pltpu
from jax.sharding import PartitionSpec as P

MESH = pl.DeviceIdType.MESH
VMEM = pl.BlockSpec(memory_space=pltpu.VMEM)
STRIP = ("col", "pair")


def place():
    return lax.axis_index("row"), lax.axis_index(STRIP)


def device_at(row, strip):
    pairs = lax.axis_size("pair")
    return (lax.axis_index("grp"), row, lax.div(strip, pairs), lax.rem(strip, pairs))


def params(number):
    return pltpu.CompilerParams(
        collective_id=number, has_side_effects=True, vmem_limit_bytes=40 * 1024 * 1024
    )


WAYS = [(a, b) for a in (-1, 0, 1) for b in (-1, 0, 1) if (a, b) != (0, 0)]


def first_kernel(
    rows, strips, cells, edge_up, kernel, pick_cols, spread_lanes,
    near, got_up, pre, gathered, shifted, block, send_sem, recv_sem, row_send, row_recv,
):
    row, strip = place()
    band, channels, width = cells.shape
    band2 = band // 4
    lanes = [pl.ds(0, width), pl.ds(width, width), pl.ds(2 * width, width)]
    tops = [pl.ds(0, 2), pl.ds(2, band), pl.ds(band + 2, 2)]

    def there(way):
        a, b = row + way[0], strip + way[1]
        return (a >= 0) & (a < rows) & (b >= 0) & (b < strips)

    barrier = pltpu.get_barrier_semaphore()
    for way in WAYS:
        if way[1] != 0:
            @pl.when(there(way))
            def _(way=way):
                pl.semaphore_signal(
                    barrier, inc=1, device_id=device_at(row + way[0], strip + way[1]), device_id_type=MESH
                )
    _, _, row_device = group("rows")
    for step in range(1, rows):
        pl.semaphore_signal(
            barrier, inc=1, device_id=row_device(lax.rem(row + step, rows)), device_id_type=MESH
        )

    def landing(way):
        return near.at[tops[way[0] + 1], :, lanes[way[1] + 1]]

    for way in WAYS:
        @pl.when(jnp.logical_not(there(way)))
        def _(way=way):
            slot = landing(way)
            slot[...] = jnp.zeros(slot.shape, slot.dtype)
            if way[0] == 0:
                slot = got_up.at[0 if way[1] < 0 else 1]
                slot[...] = jnp.zeros(slot.shape, slot.dtype)
    near[tops[1], :, lanes[1]] = cells[...]

    high = 1 + jnp.where(row > 0, 1, 0) + jnp.where(row < rows - 1, 1, 0)
    across = jnp.where(strip > 0, 1, 0) + jnp.where(strip < strips - 1, 1, 0)
    pl.semaphore_wait(barrier, high * across + rows - 1)

    def copy_to(way):
        back = (-way[0], -way[1])
        source = cells.at[[pl.ds(0, 2), pl.ds(0, band), pl.ds(band - 2, 2)][way[0] + 1]]
        return pltpu.make_async_remote_copy(
            src_ref=source,
            dst_ref=landing(back),
            send_sem=send_sem.at[WAYS.index(way)],
            recv_sem=recv_sem.at[WAYS.index(back)],
            device_id=device_at(row + way[0], strip + way[1]),
            device_id_type=MESH,
        )

    def upstream_to(way):
        side = 0 if way[1] < 0 else 1
        return pltpu.make_async_remote_copy(
            src_ref=edge_up.at[side],
            dst_ref=got_up.at[1 - side],
            send_sem=send_sem.at[8 + side],
            recv_sem=recv_sem.at[9 - side],
            device_id=device_at(row, strip + way[1]),
            device_id_type=MESH,
        )

    def arrival(way):
        back = (-way[0], -way[1])
        return pltpu.make_async_remote_copy(
            src_ref=landing(way),
            dst_ref=landing(way),
            send_sem=send_sem.at[WAYS.index(way)],
            recv_sem=recv_sem.at[WAYS.index(way)],
            device_id=device_at(row + back[0], strip + back[1]),
            device_id_type=MESH,
        )

    for way in sorted(WAYS, key=lambda w: (abs(w[0]), -abs(w[1]))):
        @pl.when(there(way))
        def _(way=way):
            copy_to(way).start()
    for way in ((0, -1), (0, 1)):
        @pl.when(there(way))
        def _(way=way):
            upstream_to(way).start()
    for way in WAYS:
        @pl.when(there(way))
        def _(way=way):
            arrival(way).wait_recv()

    full = 3 * width

    @pl.loop(0, band + 4)
    def _(h):
        here = near[h]
        wide = here.astype(jnp.float32)
        shifted[h, pl.ds(0, channels)] = pltpu.roll(wide, 1, 1).astype(jnp.bfloat16)
        shifted[h, pl.ds(channels, channels)] = here
        shifted[h, pl.ds(2 * channels, channels)] = pltpu.roll(wide, full - 1, 1).astype(jnp.bfloat16)

    @pl.loop(0, band + 2)
    def _(h):
        patches = shifted[pl.ds(h, 3)].reshape(9 * channels, full)
        pre[h] = jnp.dot(kernel[...], patches, preferred_element_type=jnp.float32)

    def silu(values):
        return values / (1.0 + jnp.exp(-values))

    contract = (((1,), (1,)), ((), ()))
    room = pick_cols.shape[0] // 2
    pooled = []
    for u in range(band2):
        total = jnp.zeros((room, 4 * channels), jnp.float32)
        for i in range(2):
            at = 1 + 4 * u + 2 * i
            pair_sum = (silu(pre[at]) + silu(pre[at + 1])) * 0.25
            upper = pair_sum.astype(jnp.bfloat16)
            lower = (pair_sum - upper.astype(jnp.float32)).astype(jnp.bfloat16)
            mean = lax.dot_general(pick_cols[...], upper, contract, preferred_element_type=jnp.float32)
            mean += lax.dot_general(pick_cols[...], lower, contract, preferred_element_type=jnp.float32)
            mean = mean.astype(jnp.bfloat16)
            for j in range(2):
                total += jnp.dot(
                    mean[j * room : (j + 1) * room],
                    spread_lanes[2 * i + j],
                    preferred_element_type=jnp.float32,
                )
        pooled.append(total)
    pooled = jnp.concatenate(pooled, 0).astype(jnp.bfloat16)
    block[...] = pooled
    finish = post(rows, row, row_device, lambda peer: block, gathered, row_send, row_recv)
    gathered[row] = pooled
    for way in WAYS:
        @pl.when(there(way))
        def _(way=way):
            copy_to(way).wait_send()
            if way[0] == 0:
                upstream_to(way).wait_send()
                upstream_to((-way[0], -way[1])).wait_recv()
    finish()


def first_layer(features_in, upstream, filters_one, number):
    channels, band, width = features_in.shape
    rows, strips = lax.axis_size("row"), lax.axis_size(STRIP)
    strip = lax.axis_index(STRIP)
    band2, width2 = band // 4, width // 4
    quads = 4 * channels
    near2 = width2 + 6
    room = -(-near2 // 16) * 16
    if (band2 * (-(-near2 // 8) * 8)) % 16 == 0:
        room = -(-near2 // 8) * 8
    height2, _, filters = upstream.shape
    cells = jnp.transpose(features_in, (1, 0, 2))
    edge_up = jnp.stack(
        [upstream[:, :2].reshape(2 * height2, filters), upstream[:, -2:].reshape(2 * height2, filters)]
    )
    v = jnp.arange(room)
    start = width + 4 * (v - 3)[None, :, None] + 2 * jnp.arange(2)[:, None, None]
    lane = jnp.arange(3 * width)[None, None, :]
    at_col = strip * width2 - 3 + v
    inside = (v < near2) & (at_col >= 0) & (at_col < width2 * strips)
    pick_cols = ((lane == start) | (lane == start + 1)) & inside[None, :, None]
    pick_cols = pick_cols.astype(jnp.bfloat16).reshape(2 * room, 3 * width)
    target = 4 * jnp.arange(channels)[None, :, None] + jnp.arange(4)[:, None, None]
    spread_lanes = (jnp.arange(quads)[None, None] == target).astype(jnp.bfloat16)
    near, got_up, pre, gathered = pl.pallas_call(
        functools.partial(first_kernel, rows, strips),
        out_shape=(
            jax.ShapeDtypeStruct((band + 4, channels, 3 * width), jnp.bfloat16),
            jax.ShapeDtypeStruct(edge_up.shape, jnp.bfloat16),
            jax.ShapeDtypeStruct((band + 2, channels, 3 * width), jnp.float32),
            jax.ShapeDtypeStruct((rows, band2 * room, quads), jnp.bfloat16),
        ),
        in_specs=[VMEM] * 5,
        out_specs=(VMEM,) * 4,
        scratch_shapes=[
            pltpu.VMEM((band + 4, 3 * channels, 3 * width), jnp.bfloat16),
            pltpu.VMEM((band2 * room, quads), jnp.bfloat16),
        ]
        + sems(10)
        + sems(rows),
        compiler_params=params(number),
    )(cells, edge_up, filters_one.reshape(channels, 9 * channels), pick_cols, spread_lanes)
    own = gathered.reshape(rows * band2, room, quads)[:, :near2]
    got_up = got_up.reshape(2, height2, 2, filters)
    inner = slice(width - 1, 2 * width + 1)
    return (
        near[1:-1, :, inner],
        pre[:, :, inner],
        own,
        jnp.concatenate([got_up[0], upstream, got_up[1]], 1),
    )


def post(count, me, device_of, source, landing, send_sem, recv_sem):
    def copy_of(step):
        peer = lax.rem(me + step, count)
        return pltpu.make_async_remote_copy(
            src_ref=source(peer),
            dst_ref=landing.at[me],
            send_sem=send_sem.at[step],
            recv_sem=recv_sem.at[me],
            device_id=device_of(peer),
            device_id_type=MESH,
        )

    def arrival(step):
        peer = lax.rem(me + step, count)
        return pltpu.make_async_remote_copy(
            src_ref=source(peer),
            dst_ref=landing.at[peer],
            send_sem=send_sem.at[step],
            recv_sem=recv_sem.at[peer],
            device_id=device_of(peer),
            device_id_type=MESH,
        )

    @pl.loop(1, count)
    def _(step):
        copy_of(step).start()

    def finish():
        @pl.loop(1, count)
        def _(step):
            copy_of(step).wait_send()
            arrival(step).wait_recv()

    return finish


def group(kind):
    rows, strips = lax.axis_size("row"), lax.axis_size(STRIP)
    row, strip = place()
    if kind == "all":
        return (
            rows * strips,
            row * strips + strip,
            lambda i: device_at(lax.div(i, strips), lax.rem(i, strips)),
        )
    if kind == "strips":
        return strips, strip, lambda i: device_at(row, i)
    return rows, row, lambda i: device_at(i, strip)


def sems(count):
    return [pltpu.SemaphoreType.DMA((count,)), pltpu.SemaphoreType.DMA((count,))]


def group_size(kind):
    rows, strips = lax.axis_size("row"), lax.axis_size(STRIP)
    return dict(all=rows * strips, strips=strips, rows=rows)[kind]


def total_of(count, landing):
    return lax.fori_loop(
        1,
        count,
        lambda i, value: value + landing[i].astype(jnp.float32),
        landing[0].astype(jnp.float32),
    )


def scatter_kernel(
    blocks, strip_map, out, maps, landing, send_sem, recv_sem, map_send, map_recv, on_send
):
    rows, me, row_device = group("rows")
    row, strip = place()
    cols, pairs = lax.axis_size("col"), lax.axis_size("pair")
    col, pair = lax.axis_index("col"), lax.axis_index("pair")

    barrier = pltpu.get_barrier_semaphore()
    for step in range(1, rows):
        pl.semaphore_signal(
            barrier, inc=1, device_id=row_device(lax.rem(me + step, rows)), device_id_type=MESH
        )
    for step in range(1, cols):
        pl.semaphore_signal(
            barrier,
            inc=1,
            device_id=device_at(row, lax.rem(col + step, cols) * pairs + pair),
            device_id_type=MESH,
        )
    for step in range(1, pairs):
        pl.semaphore_signal(
            barrier,
            inc=1,
            device_id=device_at(row, col * pairs + lax.rem(pair + step, pairs)),
            device_id_type=MESH,
        )
    pl.semaphore_wait(barrier, rows + cols + pairs - 3)

    def across(step):
        return pltpu.make_async_remote_copy(
            src_ref=strip_map,
            dst_ref=maps.at[strip],
            send_sem=map_send.at[step],
            recv_sem=map_recv.at[strip],
            device_id=device_at(row, lax.rem(col + step, cols) * pairs + pair),
            device_id_type=MESH,
        )

    def onward(source, column, step):
        slot = column * pairs + pair
        return pltpu.make_async_remote_copy(
            src_ref=source,
            dst_ref=maps.at[slot],
            send_sem=on_send.at[column * pairs + step],
            recv_sem=map_recv.at[slot],
            device_id=device_at(row, col * pairs + lax.rem(pair + step, pairs)),
            device_id_type=MESH,
        )

    def arrival(slot):
        return pltpu.make_async_remote_copy(
            src_ref=strip_map,
            dst_ref=maps.at[slot],
            send_sem=map_send.at[0],
            recv_sem=map_recv.at[slot],
            device_id=device_at(row, strip),
            device_id_type=MESH,
        )

    for step in range(1, cols):
        across(step).start()
    finish = post(rows, me, row_device, lambda peer: blocks.at[peer], landing, send_sem, recv_sem)
    for step in range(1, pairs):
        onward(strip_map, col, step).start()
    landing[me] = blocks[me]
    maps[strip] = strip_map[...]
    for step in range(1, cols):
        column = lax.rem(col + step, cols)
        slot = column * pairs + pair
        arrival(slot).wait_recv()
        for other in range(1, pairs):
            onward(maps.at[slot], column, other).start()
    finish()
    out[...] = total_of(rows, landing).astype(out.dtype)
    for step in range(1, cols):
        across(step).wait_send()
    for step in range(cols):
        column = lax.rem(col + step, cols)
        for other in range(1, pairs):
            onward(strip_map, column, other).wait_send()
            arrival(column * pairs + lax.rem(pair + other, pairs)).wait_recv()


def reduce_scatter(blocks, strip_map, number):
    rows, strips = group_size("rows"), group_size("strips")
    return pl.pallas_call(
        scatter_kernel,
        out_shape=(
            jax.ShapeDtypeStruct(blocks.shape[1:], jnp.bfloat16),
            jax.ShapeDtypeStruct((strips,) + strip_map.shape, strip_map.dtype),
        ),
        in_specs=[VMEM] * 2,
        out_specs=(VMEM,) * 2,
        scratch_shapes=[pltpu.VMEM(blocks.shape, blocks.dtype)]
        + sems(rows)
        + sems(strips)
        + [pltpu.SemaphoreType.DMA((strips,))],
        compiler_params=params(number),
    )(blocks, strip_map)


def all_reduce_kernel(blocks, out, landing, part, parts, mine, *semaphores):
    rows, row, row_device = group("rows")
    strips, strip, strip_device = group("strips")
    barrier = pltpu.get_barrier_semaphore()
    for step in range(1, rows):
        pl.semaphore_signal(
            barrier, inc=1, device_id=row_device(lax.rem(row + step, rows)), device_id_type=MESH
        )
    for step in range(1, strips):
        pl.semaphore_signal(
            barrier, inc=1, device_id=strip_device(lax.rem(strip + step, strips)), device_id_type=MESH
        )
    pl.semaphore_wait(barrier, rows + strips - 2)
    one, two, three = semaphores[:2], semaphores[2:4], semaphores[4:]
    finish = post(strips, strip, strip_device, lambda peer: blocks.at[peer], landing, *one)
    landing[strip] = blocks[strip]
    finish()
    total = total_of(strips, landing).astype(part.dtype)
    part[...] = total
    finish = post(rows, row, row_device, lambda peer: part, parts, *two)
    parts[row] = total
    finish()
    total = total_of(rows, parts).astype(part.dtype)
    mine[...] = total
    finish = post(strips, strip, strip_device, lambda peer: mine, out, *three)
    out[strip] = total
    finish()


def all_reduce(blocks, number):
    rows, strips = group_size("rows"), group_size("strips")
    piece, kind = blocks.shape[1:], blocks.dtype
    return pl.pallas_call(
        all_reduce_kernel,
        out_shape=jax.ShapeDtypeStruct(blocks.shape, kind),
        in_specs=[VMEM],
        out_specs=VMEM,
        scratch_shapes=[
            pltpu.VMEM(blocks.shape, kind),
            pltpu.VMEM(piece, kind),
            pltpu.VMEM((rows,) + piece, kind),
            pltpu.VMEM(piece, kind),
        ]
        + sems(strips)
        + sems(rows)
        + sems(strips),
        compiler_params=params(number),
    )(blocks)


def conv_valid(cells, kernel, numbers):
    return lax.conv_general_dilated(
        cells[None], kernel, (1, 1), "VALID", dimension_numbers=numbers, preferred_element_type=jnp.float32
    )[0]


def flip_kernel(kernel):
    return jnp.transpose(kernel[:, ::-1, ::-1, :], (3, 1, 2, 0))


def silu_slope(values):
    sigmoid_value = jax.nn.sigmoid(values)
    return sigmoid_value * (1.0 + values * (1.0 - sigmoid_value))


def tap_grads(gradient, padded, scale, letters, spatial):
    row_count, col_count = (gradient.shape[axis] for axis in spatial)
    taps = []
    for first in range(3):
        for second in range(3):
            window = lax.slice_in_dim(padded, first, first + row_count, axis=spatial[0])
            window = lax.slice_in_dim(window, second, second + col_count, axis=spatial[1])
            taps.append(
                jnp.einsum(letters, gradient, window, preferred_element_type=jnp.float32) * scale
            )
    return jnp.stack(taps, 1)


def local(features_in, filters_one, filters_two, out_grad):
    channels, band, width = features_in.shape
    rows, strips = lax.axis_size("row"), lax.axis_size(STRIP)
    row, strip = place()
    quads = channels * 4
    band2, width2 = band // 4, width // 4
    height2, full2 = band2 * rows, width2 * strips
    filters = filters_two.shape[0]

    near_in, pre_one, own, upstream = first_layer(
        features_in, jnp.transpose(out_grad, (2, 1, 0)), filters_one, 0
    )
    pre_two = conv_valid(
        jnp.pad(own, ((1, 1), (0, 0), (0, 0))), filters_two, ("NHWC", "OHWI", "NHWC")
    )
    near = (upstream.astype(jnp.float32) * silu_slope(pre_two)).astype(jnp.bfloat16)

    spread = conv_valid(
        jnp.pad(near, ((1, 1), (0, 0), (0, 0))), flip_kernel(filters_two), ("NHWC", "OHWI", "NHWC")
    )
    channel = jnp.arange(quads)
    low_row = (channel // 2) % 2 == 1
    low_col = channel % 2 == 1
    tall = jnp.pad(spread, ((1, 1), (0, 0), (0, 0)))
    bands = spread.reshape(rows, band2, width2 + 2, quads)
    rim = jnp.where(low_row, tall[0:height2:band2], tall[band2 + 1 : height2 + 2 : band2])
    bands = jnp.concatenate([bands, rim[:, None]], 1)
    edge = jnp.where(low_col, bands[:, :, :1], bands[:, :, -1:])
    bands = jnp.concatenate([bands[:, :, 1:-1], edge], 2).astype(jnp.bfloat16)
    spots = (band2 + 1) * (width2 + 1)
    bands = jnp.pad(bands.reshape(rows, spots, quads), ((0, 0), (0, -spots % 16), (0, 0)))
    strip_map = jnp.concatenate([own[:, 3:-3], near[:, 2:-2]], 2).reshape(height2 * width2, quads + filters)
    grad_pooled, maps = reduce_scatter(bands, strip_map, 2)

    by_part = jnp.arange(quads)
    order = 4 * (by_part % channels) + by_part // channels
    pick = (channel[:, None] == order[None]).astype(jnp.bfloat16)
    parts = jnp.dot(grad_pooled[:spots], pick, preferred_element_type=jnp.float32).astype(jnp.bfloat16)
    parts = parts.reshape(band2 + 1, width2 + 1, 2, 2, channels)
    source = (jnp.arange(width + 2) + 1) // 2
    source = jnp.where(source == 0, 2 * width2 + 1, source - 1)
    place_of = 2 * jnp.arange(width2 + 1)[:, None] + jnp.arange(2)[None]
    expand = (place_of[:, :, None] == source[None, None]).astype(jnp.bfloat16)
    halves = jnp.einsum("uvijc,vjw->uicw", parts, expand, preferred_element_type=jnp.float32)
    halves = halves.reshape(2 * band2 + 2, channels, width + 2)
    halves = jnp.concatenate([halves[-1:], halves[:-1]], 0)
    tall_grad = jnp.repeat(halves, 2, 0)[1:-1] * 0.25
    at_row = row * band - 1 + jnp.arange(band + 2)
    at_col = strip * width - 1 + jnp.arange(width + 2)
    inside = ((at_row >= 0) & (at_row < band * rows))[:, None, None] & (
        (at_col >= 0) & (at_col < width * strips)
    )
    grad_ext = jnp.where(inside, tall_grad * silu_slope(pre_one), 0.0).astype(jnp.bfloat16)

    cells = channels * 9 * channels
    scale = 1.0 / math.sqrt(band * rows * width * strips)
    local_one = tap_grads(grad_ext[1:-1, :, 1:-1], near_in, scale, "how,hcw->oc", (0, 2))
    piece = -(-cells // (strips * 128 * 16)) * 16
    flat = jnp.pad(local_one.reshape(-1).astype(jnp.bfloat16), (0, strips * piece * 128 - cells))
    summed = all_reduce(flat.reshape(strips, piece, 128), 3)
    grad_one = summed.reshape(-1)[:cells].reshape(channels, 3, 3, channels).astype(jnp.float32)

    input_grad = conv_valid(
        jnp.transpose(grad_ext, (1, 0, 2)), flip_kernel(filters_one), ("NCHW", "OHWI", "NCHW")
    ).astype(jnp.bfloat16)

    maps = jnp.transpose(maps.reshape(strips, height2, width2, quads + filters), (1, 0, 2, 3))
    maps = maps.reshape(height2, full2, quads + filters)
    whole = jnp.pad(maps[:, :, :quads], ((1, 1), (1, 1), (0, 0)))
    grad_two = tap_grads(
        maps[:, :, quads:], whole, 1.0 / math.sqrt(height2 * full2), "hwo,hwc->oc", (0, 1)
    )
    return (input_grad, grad_one, grad_two.reshape(filters, 3, 3, quads))


def solution(mesh):
    in_specs = (
        P("grp", "row", ("col", "pair")),
        P(),
        P("row", None, None, None),
        P(("grp", "row"), ("col", "pair"), None),
    )
    out_specs = (
        P("grp", "row", ("col", "pair")),
        P("grp", None, None, None),
        P(("grp", "row"), None, None, None),
    )
    return jax.shard_map(local, mesh=mesh, in_specs=in_specs, out_specs=out_specs, check_vma=False)
```

```python
import functools
import math

import jax
import jax.numpy as jnp
from jax import lax
from jax.experimental import pallas as pl
from jax.experimental.pallas import tpu as pltpu
from jax.sharding import PartitionSpec as P

MESH = pl.DeviceIdType.MESH
VMEM = pl.BlockSpec(memory_space=pltpu.VMEM)
STRIP = ("col", "pair")


def place():
    return lax.axis_index("row"), lax.axis_index(STRIP)


def device_at(row, strip):
    pairs = lax.axis_size("pair")
    return (lax.axis_index("grp"), row, lax.div(strip, pairs), lax.rem(strip, pairs))


def params(number):
    return pltpu.CompilerParams(
        collective_id=number, has_side_effects=True, vmem_limit_bytes=40 * 1024 * 1024
    )


WAYS = [(a, b) for a in (-1, 0, 1) for b in (-1, 0, 1) if (a, b) != (0, 0)]


def first_kernel(
    rows, strips, cells, edge_up, kernel, pick_cols, spread_lanes,
    got_up, pre, gathered, shifted, near, block, send_sem, recv_sem, row_send, row_recv,
):
    row, strip = place()
    band, channels, width = cells.shape
    band2 = band // 4
    lanes = [pl.ds(0, width), pl.ds(width, width), pl.ds(2 * width, width)]
    tops = [pl.ds(0, 2), pl.ds(2, band), pl.ds(band + 2, 2)]

    def there(way):
        a, b = row + way[0], strip + way[1]
        return (a >= 0) & (a < rows) & (b >= 0) & (b < strips)

    barrier = pltpu.get_barrier_semaphore()
    for way in WAYS:
        if way[1] != 0:
            @pl.when(there(way))
            def _(way=way):
                pl.semaphore_signal(
                    barrier, inc=1, device_id=device_at(row + way[0], strip + way[1]), device_id_type=MESH
                )
    _, _, row_device = group("rows")
    for step in range(1, rows):
        pl.semaphore_signal(
            barrier, inc=1, device_id=row_device(lax.rem(row + step, rows)), device_id_type=MESH
        )

    def landing(way):
        return near.at[tops[way[0] + 1], :, lanes[way[1] + 1]]

    for way in WAYS:
        @pl.when(jnp.logical_not(there(way)))
        def _(way=way):
            slot = landing(way)
            slot[...] = jnp.zeros(slot.shape, slot.dtype)
            if way[0] == 0:
                slot = got_up.at[0 if way[1] < 0 else 1]
                slot[...] = jnp.zeros(slot.shape, slot.dtype)
    near[tops[1], :, lanes[1]] = cells[...]

    high = 1 + jnp.where(row > 0, 1, 0) + jnp.where(row < rows - 1, 1, 0)
    across = jnp.where(strip > 0, 1, 0) + jnp.where(strip < strips - 1, 1, 0)
    pl.semaphore_wait(barrier, high * across + rows - 1)

    def copy_to(way):
        back = (-way[0], -way[1])
        source = cells.at[[pl.ds(0, 2), pl.ds(0, band), pl.ds(band - 2, 2)][way[0] + 1]]
        return pltpu.make_async_remote_copy(
            src_ref=source,
            dst_ref=landing(back),
            send_sem=send_sem.at[WAYS.index(way)],
            recv_sem=recv_sem.at[WAYS.index(back)],
            device_id=device_at(row + way[0], strip + way[1]),
            device_id_type=MESH,
        )

    def upstream_to(way):
        side = 0 if way[1] < 0 else 1
        return pltpu.make_async_remote_copy(
            src_ref=edge_up.at[side],
            dst_ref=got_up.at[1 - side],
            send_sem=send_sem.at[8 + side],
            recv_sem=recv_sem.at[9 - side],
            device_id=device_at(row, strip + way[1]),
            device_id_type=MESH,
        )

    def arrival(way):
        back = (-way[0], -way[1])
        return pltpu.make_async_remote_copy(
            src_ref=landing(way),
            dst_ref=landing(way),
            send_sem=send_sem.at[WAYS.index(way)],
            recv_sem=recv_sem.at[WAYS.index(way)],
            device_id=device_at(row + back[0], strip + back[1]),
            device_id_type=MESH,
        )

    for way in sorted(WAYS, key=lambda w: (abs(w[0]), -abs(w[1]))):
        @pl.when(there(way))
        def _(way=way):
            copy_to(way).start()
    for way in ((0, -1), (0, 1)):
        @pl.when(there(way))
        def _(way=way):
            upstream_to(way).start()
    for way in WAYS:
        @pl.when(there(way))
        def _(way=way):
            arrival(way).wait_recv()

    full = 3 * width

    @pl.loop(0, band + 4)
    def _(h):
        here = near[h]
        wide = here.astype(jnp.float32)
        shifted[h, pl.ds(0, channels)] = pltpu.roll(wide, 1, 1).astype(jnp.bfloat16)
        shifted[h, pl.ds(channels, channels)] = here
        shifted[h, pl.ds(2 * channels, channels)] = pltpu.roll(wide, full - 1, 1).astype(jnp.bfloat16)

    @pl.loop(0, band + 2)
    def _(h):
        patches = shifted[pl.ds(h, 3)].reshape(9 * channels, full)
        pre[h] = jnp.dot(kernel[...], patches, preferred_element_type=jnp.float32)

    def silu(values):
        return values / (1.0 + jnp.exp(-values))

    contract = (((1,), (1,)), ((), ()))
    room = pick_cols.shape[0] // 2
    pooled = []
    for u in range(band2):
        total = jnp.zeros((room, 4 * channels), jnp.float32)
        for i in range(2):
            at = 1 + 4 * u + 2 * i
            pair_sum = (silu(pre[at]) + silu(pre[at + 1])) * 0.25
            upper = pair_sum.astype(jnp.bfloat16)
            lower = (pair_sum - upper.astype(jnp.float32)).astype(jnp.bfloat16)
            mean = lax.dot_general(pick_cols[...], upper, contract, preferred_element_type=jnp.float32)
            mean += lax.dot_general(pick_cols[...], lower, contract, preferred_element_type=jnp.float32)
            mean = mean.astype(jnp.bfloat16)
            for j in range(2):
                total += jnp.dot(
                    mean[j * room : (j + 1) * room],
                    spread_lanes[2 * i + j],
                    preferred_element_type=jnp.float32,
                )
        pooled.append(total)
    pooled = jnp.concatenate(pooled, 0).astype(jnp.bfloat16)
    block[...] = pooled
    finish = post(rows, row, row_device, lambda peer: block, gathered, row_send, row_recv)
    gathered[row] = pooled
    for way in WAYS:
        @pl.when(there(way))
        def _(way=way):
            copy_to(way).wait_send()
            if way[0] == 0:
                upstream_to(way).wait_send()
                upstream_to((-way[0], -way[1])).wait_recv()
    finish()


def first_layer(features_in, upstream, filters_one, number):
    channels, band, width = features_in.shape
    rows, strips = lax.axis_size("row"), lax.axis_size(STRIP)
    strip = lax.axis_index(STRIP)
    band2, width2 = band // 4, width // 4
    quads = 4 * channels
    near2 = width2 + 6
    room = -(-near2 // 16) * 16
    if (band2 * (-(-near2 // 8) * 8)) % 16 == 0:
        room = -(-near2 // 8) * 8
    height2, _, filters = upstream.shape
    cells = jnp.transpose(features_in, (1, 0, 2))
    edge_up = jnp.stack(
        [upstream[:, :2].reshape(2 * height2, filters), upstream[:, -2:].reshape(2 * height2, filters)]
    )
    v = jnp.arange(room)
    start = width + 4 * (v - 3)[None, :, None] + 2 * jnp.arange(2)[:, None, None]
    lane = jnp.arange(3 * width)[None, None, :]
    at_col = strip * width2 - 3 + v
    inside = (v < near2) & (at_col >= 0) & (at_col < width2 * strips)
    pick_cols = ((lane == start) | (lane == start + 1)) & inside[None, :, None]
    pick_cols = pick_cols.astype(jnp.bfloat16).reshape(2 * room, 3 * width)
    target = 4 * jnp.arange(channels)[None, :, None] + jnp.arange(4)[:, None, None]
    spread_lanes = (jnp.arange(quads)[None, None] == target).astype(jnp.bfloat16)
    got_up, pre, gathered, shifted = pl.pallas_call(
        functools.partial(first_kernel, rows, strips),
        out_shape=(
            jax.ShapeDtypeStruct(edge_up.shape, jnp.bfloat16),
            jax.ShapeDtypeStruct((band + 2, channels, 3 * width), jnp.float32),
            jax.ShapeDtypeStruct((rows, band2 * room, quads), jnp.bfloat16),
            jax.ShapeDtypeStruct((band + 4, 3 * channels, 3 * width), jnp.bfloat16),
        ),
        in_specs=[VMEM] * 5,
        out_specs=(VMEM,) * 4,
        scratch_shapes=[
            pltpu.VMEM((band + 4, channels, 3 * width), jnp.bfloat16),
            pltpu.VMEM((band2 * room, quads), jnp.bfloat16),
        ]
        + sems(10)
        + sems(rows),
        compiler_params=params(number),
    )(cells, edge_up, filters_one.reshape(channels, 9 * channels), pick_cols, spread_lanes)
    own = gathered.reshape(rows * band2, room, quads)[:, :near2]
    got_up = got_up.reshape(2, height2, 2, filters)
    inner = slice(width - 1, 2 * width + 1)
    return (
        shifted,
        pre[:, :, inner],
        own,
        jnp.concatenate([got_up[0], upstream, got_up[1]], 1),
    )


def post(count, me, device_of, source, landing, send_sem, recv_sem):
    def copy_of(step):
        peer = lax.rem(me + step, count)
        return pltpu.make_async_remote_copy(
            src_ref=source(peer),
            dst_ref=landing.at[me],
            send_sem=send_sem.at[step],
            recv_sem=recv_sem.at[me],
            device_id=device_of(peer),
            device_id_type=MESH,
        )

    def arrival(step):
        peer = lax.rem(me + step, count)
        return pltpu.make_async_remote_copy(
            src_ref=source(peer),
            dst_ref=landing.at[peer],
            send_sem=send_sem.at[step],
            recv_sem=recv_sem.at[peer],
            device_id=device_of(peer),
            device_id_type=MESH,
        )

    @pl.loop(1, count)
    def _(step):
        copy_of(step).start()

    def finish():
        @pl.loop(1, count)
        def _(step):
            copy_of(step).wait_send()
            arrival(step).wait_recv()

    return finish


def group(kind):
    rows, strips = lax.axis_size("row"), lax.axis_size(STRIP)
    row, strip = place()
    if kind == "all":
        return (
            rows * strips,
            row * strips + strip,
            lambda i: device_at(lax.div(i, strips), lax.rem(i, strips)),
        )
    if kind == "strips":
        return strips, strip, lambda i: device_at(row, i)
    return rows, row, lambda i: device_at(i, strip)


def sems(count):
    return [pltpu.SemaphoreType.DMA((count,)), pltpu.SemaphoreType.DMA((count,))]


def group_size(kind):
    rows, strips = lax.axis_size("row"), lax.axis_size(STRIP)
    return dict(all=rows * strips, strips=strips, rows=rows)[kind]


def total_of(count, landing):
    return lax.fori_loop(
        1,
        count,
        lambda i, value: value + landing[i].astype(jnp.float32),
        landing[0].astype(jnp.float32),
    )


def scatter_kernel(
    blocks, strip_map, out, maps, landing, send_sem, recv_sem, map_send, map_recv, on_send
):
    rows, me, row_device = group("rows")
    row, strip = place()
    cols, pairs = lax.axis_size("col"), lax.axis_size("pair")
    col, pair = lax.axis_index("col"), lax.axis_index("pair")

    barrier = pltpu.get_barrier_semaphore()
    for step in range(1, rows):
        pl.semaphore_signal(
            barrier, inc=1, device_id=row_device(lax.rem(me + step, rows)), device_id_type=MESH
        )
    for step in range(1, cols):
        pl.semaphore_signal(
            barrier,
            inc=1,
            device_id=device_at(row, lax.rem(col + step, cols) * pairs + pair),
            device_id_type=MESH,
        )
    for step in range(1, pairs):
        pl.semaphore_signal(
            barrier,
            inc=1,
            device_id=device_at(row, col * pairs + lax.rem(pair + step, pairs)),
            device_id_type=MESH,
        )
    pl.semaphore_wait(barrier, rows + cols + pairs - 3)

    def across(step):
        return pltpu.make_async_remote_copy(
            src_ref=strip_map,
            dst_ref=maps.at[strip],
            send_sem=map_send.at[step],
            recv_sem=map_recv.at[strip],
            device_id=device_at(row, lax.rem(col + step, cols) * pairs + pair),
            device_id_type=MESH,
        )

    def onward(source, column, step):
        slot = column * pairs + pair
        return pltpu.make_async_remote_copy(
            src_ref=source,
            dst_ref=maps.at[slot],
            send_sem=on_send.at[column * pairs + step],
            recv_sem=map_recv.at[slot],
            device_id=device_at(row, col * pairs + lax.rem(pair + step, pairs)),
            device_id_type=MESH,
        )

    def arrival(slot):
        return pltpu.make_async_remote_copy(
            src_ref=strip_map,
            dst_ref=maps.at[slot],
            send_sem=map_send.at[0],
            recv_sem=map_recv.at[slot],
            device_id=device_at(row, strip),
            device_id_type=MESH,
        )

    for step in range(1, cols):
        across(step).start()
    finish = post(rows, me, row_device, lambda peer: blocks.at[peer], landing, send_sem, recv_sem)
    for step in range(1, pairs):
        onward(strip_map, col, step).start()
    landing[me] = blocks[me]
    maps[strip] = strip_map[...]
    for step in range(1, cols):
        column = lax.rem(col + step, cols)
        slot = column * pairs + pair
        arrival(slot).wait_recv()
        for other in range(1, pairs):
            onward(maps.at[slot], column, other).start()
    finish()
    out[...] = total_of(rows, landing).astype(out.dtype)
    for step in range(1, cols):
        across(step).wait_send()
    for step in range(cols):
        column = lax.rem(col + step, cols)
        for other in range(1, pairs):
            onward(strip_map, column, other).wait_send()
            arrival(column * pairs + lax.rem(pair + other, pairs)).wait_recv()


def reduce_scatter(blocks, strip_map, number):
    rows, strips = group_size("rows"), group_size("strips")
    return pl.pallas_call(
        scatter_kernel,
        out_shape=(
            jax.ShapeDtypeStruct(blocks.shape[1:], jnp.bfloat16),
            jax.ShapeDtypeStruct((strips,) + strip_map.shape, strip_map.dtype),
        ),
        in_specs=[VMEM] * 2,
        out_specs=(VMEM,) * 2,
        scratch_shapes=[pltpu.VMEM(blocks.shape, blocks.dtype)]
        + sems(rows)
        + sems(strips)
        + [pltpu.SemaphoreType.DMA((strips,))],
        compiler_params=params(number),
    )(blocks, strip_map)


def last_kernel(
    scale, shifted, gradient, grad_two_in, whole, out, taps, blocks, landing, part, parts, mine, *semaphores
):
    rows, row, row_device = group("rows")
    strips, strip, strip_device = group("strips")
    barrier = pltpu.get_barrier_semaphore()
    for step in range(1, rows):
        pl.semaphore_signal(
            barrier, inc=1, device_id=row_device(lax.rem(row + step, rows)), device_id_type=MESH
        )
    for step in range(1, strips):
        pl.semaphore_signal(
            barrier, inc=1, device_id=strip_device(lax.rem(strip + step, strips)), device_id_type=MESH
        )
    band, channels, width = gradient.shape
    steps, _, spots = grad_two_in.shape
    full2 = whole.shape[1] - 2
    chunk = spots // full2
    quads = whole.shape[2]

    def one_row(h, total):
        patches = shifted[pl.ds(h + 1, 3), :, pl.ds(width, width)].reshape(9 * channels, width)
        return total + lax.dot_general(
            gradient[h], patches, (((1,), (1,)), ((), ())), preferred_element_type=jnp.float32
        )

    total = lax.fori_loop(0, band, one_row, jnp.zeros((channels, 9 * channels), jnp.float32))
    height = channels // strips
    for peer in range(strips):
        blocks[peer] = total[peer * height : (peer + 1) * height].astype(blocks.dtype)

    def tap(index):
        first, second = divmod(index, 3)

        def product(step):
            window = whole[pl.ds(step * chunk + first, chunk), pl.ds(second, full2)]
            return scale * jnp.dot(
                grad_two_in[step], window.reshape(spots, quads), preferred_element_type=jnp.float32
            )

        taps[index] = product(0)
        if steps > 1:
            @pl.loop(1, steps)
            def _(step):
                taps[index] += product(step)

    pl.semaphore_wait(barrier, rows + strips - 2)
    one, two, three = semaphores[:2], semaphores[2:4], semaphores[4:]
    finish = post(strips, strip, strip_device, lambda peer: blocks.at[peer], landing, *one)
    landing[strip] = blocks[strip]
    for index in range(3):
        tap(index)
    finish()
    total = total_of(strips, landing).astype(part.dtype)
    part[...] = total
    finish = post(rows, row, row_device, lambda peer: part, parts, *two)
    parts[row] = total
    for index in range(3, 6):
        tap(index)
    finish()
    total = total_of(rows, parts).astype(part.dtype)
    mine[...] = total
    finish = post(strips, strip, strip_device, lambda peer: mine, out, *three)
    out[strip] = total
    for index in range(6, 9):
        tap(index)
    finish()


def last_layer(shifted, gradient, grad_two_in, whole, scale, number):
    rows, strips = group_size("rows"), group_size("strips")
    channels = gradient.shape[1]
    kind = jnp.bfloat16
    piece = (channels // strips, 9 * channels)
    return pl.pallas_call(
        functools.partial(last_kernel, scale),
        out_shape=(
            jax.ShapeDtypeStruct((strips,) + piece, kind),
            jax.ShapeDtypeStruct((9, grad_two_in.shape[1], whole.shape[2]), jnp.float32),
        ),
        in_specs=[VMEM] * 4,
        out_specs=(VMEM,) * 2,
        scratch_shapes=[
            pltpu.VMEM((strips,) + piece, kind),
            pltpu.VMEM((strips,) + piece, kind),
            pltpu.VMEM(piece, kind),
            pltpu.VMEM((rows,) + piece, kind),
            pltpu.VMEM(piece, kind),
        ]
        + sems(strips)
        + sems(rows)
        + sems(strips),
        compiler_params=params(number),
    )(shifted, gradient, grad_two_in, whole)


def conv_valid(cells, kernel, numbers):
    return lax.conv_general_dilated(
        cells[None], kernel, (1, 1), "VALID", dimension_numbers=numbers, preferred_element_type=jnp.float32
    )[0]


def flip_kernel(kernel):
    return jnp.transpose(kernel[:, ::-1, ::-1, :], (3, 1, 2, 0))


def silu_slope(values):
    sigmoid_value = jax.nn.sigmoid(values)
    return sigmoid_value * (1.0 + values * (1.0 - sigmoid_value))


def local(features_in, filters_one, filters_two, out_grad):
    channels, band, width = features_in.shape
    rows, strips = lax.axis_size("row"), lax.axis_size(STRIP)
    row, strip = place()
    quads = channels * 4
    band2, width2 = band // 4, width // 4
    height2, full2 = band2 * rows, width2 * strips
    filters = filters_two.shape[0]

    shifted, pre_one, own, upstream = first_layer(
        features_in, jnp.transpose(out_grad, (2, 1, 0)), filters_one, 0
    )
    pre_two = conv_valid(
        jnp.pad(own, ((1, 1), (0, 0), (0, 0))), filters_two, ("NHWC", "OHWI", "NHWC")
    )
    near = (upstream.astype(jnp.float32) * silu_slope(pre_two)).astype(jnp.bfloat16)

    spread = conv_valid(
        jnp.pad(near, ((1, 1), (0, 0), (0, 0))), flip_kernel(filters_two), ("NHWC", "OHWI", "NHWC")
    )
    channel = jnp.arange(quads)
    low_row = (channel // 2) % 2 == 1
    low_col = channel % 2 == 1
    tall = jnp.pad(spread, ((1, 1), (0, 0), (0, 0)))
    bands = spread.reshape(rows, band2, width2 + 2, quads)
    rim = jnp.where(low_row, tall[0:height2:band2], tall[band2 + 1 : height2 + 2 : band2])
    bands = jnp.concatenate([bands, rim[:, None]], 1)
    edge = jnp.where(low_col, bands[:, :, :1], bands[:, :, -1:])
    bands = jnp.concatenate([bands[:, :, 1:-1], edge], 2).astype(jnp.bfloat16)
    spots = (band2 + 1) * (width2 + 1)
    bands = jnp.pad(bands.reshape(rows, spots, quads), ((0, 0), (0, -spots % 16), (0, 0)))
    strip_map = jnp.concatenate([own[:, 3:-3], near[:, 2:-2]], 2).reshape(height2 * width2, quads + filters)
    grad_pooled, maps = reduce_scatter(bands, strip_map, 2)

    by_part = jnp.arange(quads)
    order = 4 * (by_part % channels) + by_part // channels
    pick = (channel[:, None] == order[None]).astype(jnp.bfloat16)
    parts = jnp.dot(grad_pooled[:spots], pick, preferred_element_type=jnp.float32).astype(jnp.bfloat16)
    parts = parts.reshape(band2 + 1, width2 + 1, 2, 2, channels)
    source = (jnp.arange(width + 2) + 1) // 2
    source = jnp.where(source == 0, 2 * width2 + 1, source - 1)
    place_of = 2 * jnp.arange(width2 + 1)[:, None] + jnp.arange(2)[None]
    expand = (place_of[:, :, None] == source[None, None]).astype(jnp.bfloat16)
    halves = jnp.einsum("uvijc,vjw->uicw", parts, expand, preferred_element_type=jnp.float32)
    halves = halves.reshape(2 * band2 + 2, channels, width + 2)
    halves = jnp.concatenate([halves[-1:], halves[:-1]], 0)
    tall_grad = jnp.repeat(halves, 2, 0)[1:-1] * 0.25
    at_row = row * band - 1 + jnp.arange(band + 2)
    at_col = strip * width - 1 + jnp.arange(width + 2)
    inside = ((at_row >= 0) & (at_row < band * rows))[:, None, None] & (
        (at_col >= 0) & (at_col < width * strips)
    )
    grad_ext = jnp.where(inside, tall_grad * silu_slope(pre_one), 0.0).astype(jnp.bfloat16)

    maps = jnp.transpose(maps.reshape(strips, height2, width2, quads + filters), (1, 0, 2, 3))
    maps = maps.reshape(height2, full2, quads + filters)
    whole = jnp.pad(maps[:, :, :quads], ((1, 1), (1, 1), (0, 0)))
    chunk = max(1, 1024 // full2)
    grad_two_in = maps[:, :, quads:].reshape(height2 // chunk, chunk * full2, filters)
    summed, taps = last_layer(
        shifted,
        grad_ext[1:-1, :, 1:-1],
        jnp.transpose(grad_two_in, (0, 2, 1)),
        whole,
        1.0 / math.sqrt(height2 * full2),
        3,
    )
    scale = 1.0 / math.sqrt(band * rows * width * strips)
    grad_one = summed.astype(jnp.float32).reshape(channels, 3, 3, channels) * scale
    grad_two = jnp.transpose(taps, (1, 0, 2)).reshape(filters, 3, 3, quads)

    input_grad = conv_valid(
        jnp.transpose(grad_ext, (1, 0, 2)), flip_kernel(filters_one), ("NCHW", "OHWI", "NCHW")
    ).astype(jnp.bfloat16)

    return (input_grad, grad_one, grad_two)


def solution(mesh):
    in_specs = (
        P("grp", "row", ("col", "pair")),
        P(),
        P("row", None, None, None),
        P(("grp", "row"), ("col", "pair"), None),
    )
    out_specs = (
        P("grp", "row", ("col", "pair")),
        P("grp", None, None, None),
        P(("grp", "row"), None, None, None),
    )
    return jax.shard_map(local, mesh=mesh, in_specs=in_specs, out_specs=out_specs, check_vma=False)
```

```python
import functools
import math

import jax
import jax.numpy as jnp
from jax import lax
from jax.experimental import pallas as pl
from jax.experimental.pallas import tpu as pltpu
from jax.sharding import PartitionSpec as P

MESH = pl.DeviceIdType.MESH
VMEM = pl.BlockSpec(memory_space=pltpu.VMEM)
STRIP = ("col", "pair")


def place():
    return lax.axis_index("row"), lax.axis_index(STRIP)


def device_at(row, strip):
    pairs = lax.axis_size("pair")
    return (lax.axis_index("grp"), row, lax.div(strip, pairs), lax.rem(strip, pairs))


def params(number):
    share = max(1, lax.axis_size("row") * lax.axis_size(STRIP) // 64)
    return pltpu.CompilerParams(
        collective_id=number, has_side_effects=True, vmem_limit_bytes=share * 12 * 1024 * 1024
    )


WAYS = [(a, b) for a in (-1, 0, 1) for b in (-1, 0, 1) if (a, b) != (0, 0)]


def first_kernel(
    rows, strips, cells, edge_up, kernel, pick_cols, spread_lanes,
    got_up, pre, gathered, shifted, near, block, send_sem, recv_sem, row_send, row_recv,
):
    row, strip = place()
    band, channels, width = cells.shape
    band2 = band // 4
    lanes = [pl.ds(0, width), pl.ds(width, width), pl.ds(2 * width, width)]
    tops = [pl.ds(0, 2), pl.ds(2, band), pl.ds(band + 2, 2)]

    def there(way):
        a, b = row + way[0], strip + way[1]
        return (a >= 0) & (a < rows) & (b >= 0) & (b < strips)

    barrier = pltpu.get_barrier_semaphore()
    for way in WAYS:
        if way[1] != 0:
            @pl.when(there(way))
            def _(way=way):
                pl.semaphore_signal(
                    barrier, inc=1, device_id=device_at(row + way[0], strip + way[1]), device_id_type=MESH
                )
    _, _, row_device = group("rows")
    for step in range(1, rows):
        pl.semaphore_signal(
            barrier, inc=1, device_id=row_device(lax.rem(row + step, rows)), device_id_type=MESH
        )

    def landing(way):
        return near.at[tops[way[0] + 1], :, lanes[way[1] + 1]]

    for way in WAYS:
        @pl.when(jnp.logical_not(there(way)))
        def _(way=way):
            slot = landing(way)
            slot[...] = jnp.zeros(slot.shape, slot.dtype)
            if way[0] == 0:
                slot = got_up.at[0 if way[1] < 0 else 1]
                slot[...] = jnp.zeros(slot.shape, slot.dtype)
    near[tops[1], :, lanes[1]] = cells[...]

    high = 1 + jnp.where(row > 0, 1, 0) + jnp.where(row < rows - 1, 1, 0)
    across = jnp.where(strip > 0, 1, 0) + jnp.where(strip < strips - 1, 1, 0)
    pl.semaphore_wait(barrier, high * across + rows - 1)

    def copy_to(way):
        back = (-way[0], -way[1])
        source = cells.at[[pl.ds(0, 2), pl.ds(0, band), pl.ds(band - 2, 2)][way[0] + 1]]
        return pltpu.make_async_remote_copy(
            src_ref=source,
            dst_ref=landing(back),
            send_sem=send_sem.at[WAYS.index(way)],
            recv_sem=recv_sem.at[WAYS.index(back)],
            device_id=device_at(row + way[0], strip + way[1]),
            device_id_type=MESH,
        )

    def upstream_to(way):
        side = 0 if way[1] < 0 else 1
        return pltpu.make_async_remote_copy(
            src_ref=edge_up.at[side],
            dst_ref=got_up.at[1 - side],
            send_sem=send_sem.at[8 + side],
            recv_sem=recv_sem.at[9 - side],
            device_id=device_at(row, strip + way[1]),
            device_id_type=MESH,
        )

    def arrival(way):
        back = (-way[0], -way[1])
        return pltpu.make_async_remote_copy(
            src_ref=landing(way),
            dst_ref=landing(way),
            send_sem=send_sem.at[WAYS.index(way)],
            recv_sem=recv_sem.at[WAYS.index(way)],
            device_id=device_at(row + back[0], strip + back[1]),
            device_id_type=MESH,
        )

    for way in sorted(WAYS, key=lambda w: (abs(w[0]), -abs(w[1]))):
        @pl.when(there(way))
        def _(way=way):
            copy_to(way).start()
    for way in ((0, -1), (0, 1)):
        @pl.when(there(way))
        def _(way=way):
            upstream_to(way).start()
    for way in WAYS:
        @pl.when(there(way))
        def _(way=way):
            arrival(way).wait_recv()

    full = 3 * width

    @pl.loop(0, band + 4)
    def _(h):
        here = near[h]
        wide = here.astype(jnp.float32)
        shifted[h, pl.ds(0, channels)] = pltpu.roll(wide, 1, 1).astype(jnp.bfloat16)
        shifted[h, pl.ds(channels, channels)] = here
        shifted[h, pl.ds(2 * channels, channels)] = pltpu.roll(wide, full - 1, 1).astype(jnp.bfloat16)

    @pl.loop(0, band + 2)
    def _(h):
        patches = shifted[pl.ds(h, 3)].reshape(9 * channels, full)
        pre[h] = jnp.dot(kernel[...], patches, preferred_element_type=jnp.float32)

    def silu(values):
        return values / (1.0 + jnp.exp(-values))

    contract = (((1,), (1,)), ((), ()))
    room = pick_cols.shape[0] // 2
    pooled = []
    for u in range(band2):
        total = jnp.zeros((room, 4 * channels), jnp.float32)
        for i in range(2):
            at = 1 + 4 * u + 2 * i
            pair_sum = (silu(pre[at]) + silu(pre[at + 1])) * 0.25
            upper = pair_sum.astype(jnp.bfloat16)
            lower = (pair_sum - upper.astype(jnp.float32)).astype(jnp.bfloat16)
            mean = lax.dot_general(pick_cols[...], upper, contract, preferred_element_type=jnp.float32)
            mean += lax.dot_general(pick_cols[...], lower, contract, preferred_element_type=jnp.float32)
            mean = mean.astype(jnp.bfloat16)
            for j in range(2):
                total += jnp.dot(
                    mean[j * room : (j + 1) * room],
                    spread_lanes[2 * i + j],
                    preferred_element_type=jnp.float32,
                )
        pooled.append(total)
    pooled = jnp.concatenate(pooled, 0).astype(jnp.bfloat16)
    block[...] = pooled
    finish = post(rows, row, row_device, lambda peer: block, gathered, row_send, row_recv)
    gathered[row] = pooled
    for way in WAYS:
        @pl.when(there(way))
        def _(way=way):
            copy_to(way).wait_send()
            if way[0] == 0:
                upstream_to(way).wait_send()
                upstream_to((-way[0], -way[1])).wait_recv()
    finish()


def first_layer(features_in, upstream, filters_one, number):
    channels, band, width = features_in.shape
    rows, strips = lax.axis_size("row"), lax.axis_size(STRIP)
    strip = lax.axis_index(STRIP)
    band2, width2 = band // 4, width // 4
    quads = 4 * channels
    near2 = width2 + 6
    room = -(-near2 // 16) * 16
    if (band2 * (-(-near2 // 8) * 8)) % 16 == 0:
        room = -(-near2 // 8) * 8
    height2, _, filters = upstream.shape
    cells = jnp.transpose(features_in, (1, 0, 2))
    edge_up = jnp.stack(
        [upstream[:, :2].reshape(2 * height2, filters), upstream[:, -2:].reshape(2 * height2, filters)]
    )
    v = jnp.arange(room)
    start = width + 4 * (v - 3)[None, :, None] + 2 * jnp.arange(2)[:, None, None]
    lane = jnp.arange(3 * width)[None, None, :]
    at_col = strip * width2 - 3 + v
    inside = (v < near2) & (at_col >= 0) & (at_col < width2 * strips)
    pick_cols = ((lane == start) | (lane == start + 1)) & inside[None, :, None]
    pick_cols = pick_cols.astype(jnp.bfloat16).reshape(2 * room, 3 * width)
    target = 4 * jnp.arange(channels)[None, :, None] + jnp.arange(4)[:, None, None]
    spread_lanes = (jnp.arange(quads)[None, None] == target).astype(jnp.bfloat16)
    got_up, pre, gathered, shifted = pl.pallas_call(
        functools.partial(first_kernel, rows, strips),
        out_shape=(
            jax.ShapeDtypeStruct(edge_up.shape, jnp.bfloat16),
            jax.ShapeDtypeStruct((band + 2, channels, 3 * width), jnp.float32),
            jax.ShapeDtypeStruct((rows, band2 * room, quads), jnp.bfloat16),
            jax.ShapeDtypeStruct((band + 4, 3 * channels, 3 * width), jnp.bfloat16),
        ),
        in_specs=[VMEM] * 5,
        out_specs=(VMEM,) * 4,
        scratch_shapes=[
            pltpu.VMEM((band + 4, channels, 3 * width), jnp.bfloat16),
            pltpu.VMEM((band2 * room, quads), jnp.bfloat16),
        ]
        + sems(10)
        + sems(rows),
        compiler_params=params(number),
    )(cells, edge_up, filters_one.reshape(channels, 9 * channels), pick_cols, spread_lanes)
    own = gathered.reshape(rows * band2, room, quads)[:, :near2]
    got_up = got_up.reshape(2, height2, 2, filters)
    inner = slice(width - 1, 2 * width + 1)
    return (
        shifted,
        pre[:, :, inner],
        own,
        jnp.concatenate([got_up[0], upstream, got_up[1]], 1),
    )


def post(count, me, device_of, source, landing, send_sem, recv_sem):
    def copy_of(step):
        peer = lax.rem(me + step, count)
        return pltpu.make_async_remote_copy(
            src_ref=source(peer),
            dst_ref=landing.at[me],
            send_sem=send_sem.at[step],
            recv_sem=recv_sem.at[me],
            device_id=device_of(peer),
            device_id_type=MESH,
        )

    def arrival(step):
        peer = lax.rem(me + step, count)
        return pltpu.make_async_remote_copy(
            src_ref=source(peer),
            dst_ref=landing.at[peer],
            send_sem=send_sem.at[step],
            recv_sem=recv_sem.at[peer],
            device_id=device_of(peer),
            device_id_type=MESH,
        )

    @pl.loop(1, count)
    def _(step):
        copy_of(step).start()

    def finish():
        @pl.loop(1, count)
        def _(step):
            copy_of(step).wait_send()
            arrival(step).wait_recv()

    return finish


def group(kind):
    rows, strips = lax.axis_size("row"), lax.axis_size(STRIP)
    row, strip = place()
    if kind == "all":
        return (
            rows * strips,
            row * strips + strip,
            lambda i: device_at(lax.div(i, strips), lax.rem(i, strips)),
        )
    if kind == "strips":
        return strips, strip, lambda i: device_at(row, i)
    return rows, row, lambda i: device_at(i, strip)


def sems(count):
    return [pltpu.SemaphoreType.DMA((count,)), pltpu.SemaphoreType.DMA((count,))]


def group_size(kind):
    rows, strips = lax.axis_size("row"), lax.axis_size(STRIP)
    return dict(all=rows * strips, strips=strips, rows=rows)[kind]


def total_of(count, landing):
    return lax.fori_loop(
        1,
        count,
        lambda i, value: value + landing[i].astype(jnp.float32),
        landing[0].astype(jnp.float32),
    )


def scatter_kernel(
    blocks, strip_map, out, maps, landing, send_sem, recv_sem, map_send, map_recv, on_send
):
    rows, me, row_device = group("rows")
    row, strip = place()
    cols, pairs = lax.axis_size("col"), lax.axis_size("pair")
    col, pair = lax.axis_index("col"), lax.axis_index("pair")

    barrier = pltpu.get_barrier_semaphore()
    for step in range(1, rows):
        pl.semaphore_signal(
            barrier, inc=1, device_id=row_device(lax.rem(me + step, rows)), device_id_type=MESH
        )
    for step in range(1, cols):
        pl.semaphore_signal(
            barrier,
            inc=1,
            device_id=device_at(row, lax.rem(col + step, cols) * pairs + pair),
            device_id_type=MESH,
        )
    for step in range(1, pairs):
        pl.semaphore_signal(
            barrier,
            inc=1,
            device_id=device_at(row, col * pairs + lax.rem(pair + step, pairs)),
            device_id_type=MESH,
        )
    pl.semaphore_wait(barrier, rows + cols + pairs - 3)

    def across(step):
        return pltpu.make_async_remote_copy(
            src_ref=strip_map,
            dst_ref=maps.at[strip],
            send_sem=map_send.at[step],
            recv_sem=map_recv.at[strip],
            device_id=device_at(row, lax.rem(col + step, cols) * pairs + pair),
            device_id_type=MESH,
        )

    def onward(source, column, step):
        slot = column * pairs + pair
        return pltpu.make_async_remote_copy(
            src_ref=source,
            dst_ref=maps.at[slot],
            send_sem=on_send.at[column * pairs + step],
            recv_sem=map_recv.at[slot],
            device_id=device_at(row, col * pairs + lax.rem(pair + step, pairs)),
            device_id_type=MESH,
        )

    def arrival(slot):
        return pltpu.make_async_remote_copy(
            src_ref=strip_map,
            dst_ref=maps.at[slot],
            send_sem=map_send.at[0],
            recv_sem=map_recv.at[slot],
            device_id=device_at(row, strip),
            device_id_type=MESH,
        )

    for step in range(1, cols):
        across(step).start()
    finish = post(rows, me, row_device, lambda peer: blocks.at[peer], landing, send_sem, recv_sem)
    for step in range(1, pairs):
        onward(strip_map, col, step).start()
    landing[me] = blocks[me]
    maps[strip] = strip_map[...]
    for step in range(1, cols):
        column = lax.rem(col + step, cols)
        slot = column * pairs + pair
        arrival(slot).wait_recv()
        for other in range(1, pairs):
            onward(maps.at[slot], column, other).start()
    finish()
    out[...] = total_of(rows, landing).astype(out.dtype)
    for step in range(1, cols):
        across(step).wait_send()
    for step in range(cols):
        column = lax.rem(col + step, cols)
        for other in range(1, pairs):
            onward(strip_map, column, other).wait_send()
            arrival(column * pairs + lax.rem(pair + other, pairs)).wait_recv()


def reduce_scatter(blocks, strip_map, number):
    rows, strips = group_size("rows"), group_size("strips")
    return pl.pallas_call(
        scatter_kernel,
        out_shape=(
            jax.ShapeDtypeStruct(blocks.shape[1:], jnp.bfloat16),
            jax.ShapeDtypeStruct((strips,) + strip_map.shape, strip_map.dtype),
        ),
        in_specs=[VMEM] * 2,
        out_specs=(VMEM,) * 2,
        scratch_shapes=[pltpu.VMEM(blocks.shape, blocks.dtype)]
        + sems(rows)
        + sems(strips)
        + [pltpu.SemaphoreType.DMA((strips,))],
        compiler_params=params(number),
    )(blocks, strip_map)


def last_kernel(
    scale, shifted, gradient, maps, whole, out, taps, turned, blocks, landing, part, parts, mine, *semaphores
):
    rows, row, row_device = group("rows")
    strips, strip, strip_device = group("strips")
    barrier = pltpu.get_barrier_semaphore()
    for step in range(1, rows):
        pl.semaphore_signal(
            barrier, inc=1, device_id=row_device(lax.rem(row + step, rows)), device_id_type=MESH
        )
    for step in range(1, strips):
        pl.semaphore_signal(
            barrier, inc=1, device_id=strip_device(lax.rem(strip + step, strips)), device_id_type=MESH
        )
    band, channels, width = gradient.shape
    steps, filters, spots = turned.shape
    full2 = whole.shape[1] - 2
    chunk = spots // full2
    quads = whole.shape[2]

    def one_row(h, total):
        patches = shifted[pl.ds(h + 1, 3), :, pl.ds(width, width)].reshape(9 * channels, width)
        return total + lax.dot_general(
            gradient[h], patches, (((1,), (1,)), ((), ())), preferred_element_type=jnp.float32
        )

    total = lax.fori_loop(0, band, one_row, jnp.zeros((channels, 9 * channels), jnp.float32))
    height = channels // strips
    for peer in range(strips):
        blocks[peer] = total[peer * height : (peer + 1) * height].astype(blocks.dtype)

    for step in range(steps):
        rows_of = maps[pl.ds(step * chunk, chunk), :, pl.ds(quads, filters)].reshape(spots, filters)
        turned[step] = rows_of.astype(jnp.float32).T.astype(turned.dtype)

    def tap(index):
        first, second = divmod(index, 3)

        def product(step):
            window = whole[pl.ds(step * chunk + first, chunk), pl.ds(second, full2)]
            return scale * jnp.dot(
                turned[step], window.reshape(spots, quads), preferred_element_type=jnp.float32
            )

        taps[index] = product(0)
        if steps > 1:
            @pl.loop(1, steps)
            def _(step):
                taps[index] += product(step)

    pl.semaphore_wait(barrier, rows + strips - 2)
    one, two, three = semaphores[:2], semaphores[2:4], semaphores[4:]
    finish = post(strips, strip, strip_device, lambda peer: blocks.at[peer], landing, *one)
    landing[strip] = blocks[strip]
    for index in range(3):
        tap(index)
    finish()
    total = total_of(strips, landing).astype(part.dtype)
    part[...] = total
    finish = post(rows, row, row_device, lambda peer: part, parts, *two)
    parts[row] = total
    for index in range(3, 6):
        tap(index)
    finish()
    total = total_of(rows, parts).astype(part.dtype)
    mine[...] = total
    finish = post(strips, strip, strip_device, lambda peer: mine, out, *three)
    out[strip] = total
    for index in range(6, 9):
        tap(index)
    finish()


def last_layer(shifted, gradient, maps, whole, scale, number):
    rows, strips = group_size("rows"), group_size("strips")
    channels = gradient.shape[1]
    kind = jnp.bfloat16
    height2, full2, depth = maps.shape
    filters = depth - whole.shape[2]
    chunk = max(1, 1024 // full2)
    piece = (channels // strips, 9 * channels)
    return pl.pallas_call(
        functools.partial(last_kernel, scale),
        out_shape=(
            jax.ShapeDtypeStruct((strips,) + piece, kind),
            jax.ShapeDtypeStruct((9, filters, whole.shape[2]), jnp.float32),
        ),
        in_specs=[VMEM] * 4,
        out_specs=(VMEM,) * 2,
        scratch_shapes=[
            pltpu.VMEM((height2 // chunk, filters, chunk * full2), kind),
            pltpu.VMEM((strips,) + piece, kind),
            pltpu.VMEM((strips,) + piece, kind),
            pltpu.VMEM(piece, kind),
            pltpu.VMEM((rows,) + piece, kind),
            pltpu.VMEM(piece, kind),
        ]
        + sems(strips)
        + sems(rows)
        + sems(strips),
        compiler_params=params(number),
    )(shifted, gradient, maps, whole)


def conv_valid(cells, kernel, numbers):
    return lax.conv_general_dilated(
        cells[None], kernel, (1, 1), "VALID", dimension_numbers=numbers, preferred_element_type=jnp.float32
    )[0]


def flip_kernel(kernel):
    return jnp.transpose(kernel[:, ::-1, ::-1, :], (3, 1, 2, 0))


def silu_slope(values):
    sigmoid_value = jax.nn.sigmoid(values)
    return sigmoid_value * (1.0 + values * (1.0 - sigmoid_value))


def local(features_in, filters_one, filters_two, out_grad):
    channels, band, width = features_in.shape
    rows, strips = lax.axis_size("row"), lax.axis_size(STRIP)
    row, strip = place()
    quads = channels * 4
    band2, width2 = band // 4, width // 4
    height2, full2 = band2 * rows, width2 * strips
    filters = filters_two.shape[0]

    shifted, pre_one, own, upstream = first_layer(
        features_in, jnp.transpose(out_grad, (2, 1, 0)), filters_one, 0
    )
    pre_two = conv_valid(
        jnp.pad(own, ((1, 1), (0, 0), (0, 0))), filters_two, ("NHWC", "OHWI", "NHWC")
    )
    near = (upstream.astype(jnp.float32) * silu_slope(pre_two)).astype(jnp.bfloat16)

    spread = conv_valid(
        jnp.pad(near, ((1, 1), (0, 0), (0, 0))), flip_kernel(filters_two), ("NHWC", "OHWI", "NHWC")
    )
    channel = jnp.arange(quads)
    low_row = (channel // 2) % 2 == 1
    low_col = channel % 2 == 1
    tall = jnp.pad(spread, ((1, 1), (0, 0), (0, 0)))
    bands = spread.reshape(rows, band2, width2 + 2, quads)
    rim = jnp.where(low_row, tall[0:height2:band2], tall[band2 + 1 : height2 + 2 : band2])
    bands = jnp.concatenate([bands, rim[:, None]], 1)
    edge = jnp.where(low_col, bands[:, :, :1], bands[:, :, -1:])
    bands = jnp.concatenate([bands[:, :, 1:-1], edge], 2).astype(jnp.bfloat16)
    spots = (band2 + 1) * (width2 + 1)
    bands = jnp.pad(bands.reshape(rows, spots, quads), ((0, 0), (0, -spots % 16), (0, 0)))
    strip_map = jnp.concatenate([own[:, 3:-3], near[:, 2:-2]], 2).reshape(height2 * width2, quads + filters)
    grad_pooled, maps = reduce_scatter(bands, strip_map, 2)

    by_part = jnp.arange(quads)
    order = 4 * (by_part % channels) + by_part // channels
    pick = (channel[:, None] == order[None]).astype(jnp.bfloat16)
    parts = jnp.dot(grad_pooled[:spots], pick, preferred_element_type=jnp.float32).astype(jnp.bfloat16)
    parts = parts.reshape(band2 + 1, width2 + 1, 2, 2, channels)
    source = (jnp.arange(width + 2) + 1) // 2
    source = jnp.where(source == 0, 2 * width2 + 1, source - 1)
    place_of = 2 * jnp.arange(width2 + 1)[:, None] + jnp.arange(2)[None]
    expand = (place_of[:, :, None] == source[None, None]).astype(jnp.bfloat16)
    halves = jnp.einsum("uvijc,vjw->uicw", parts, expand, preferred_element_type=jnp.float32)
    halves = halves.reshape(2 * band2 + 2, channels, width + 2)
    halves = jnp.concatenate([halves[-1:], halves[:-1]], 0)
    tall_grad = jnp.repeat(halves, 2, 0)[1:-1] * 0.25
    at_row = row * band - 1 + jnp.arange(band + 2)
    at_col = strip * width - 1 + jnp.arange(width + 2)
    inside = ((at_row >= 0) & (at_row < band * rows))[:, None, None] & (
        (at_col >= 0) & (at_col < width * strips)
    )
    grad_ext = jnp.where(inside, tall_grad * silu_slope(pre_one), 0.0).astype(jnp.bfloat16)

    maps = jnp.transpose(maps.reshape(strips, height2, width2, quads + filters), (1, 0, 2, 3))
    maps = maps.reshape(height2, full2, quads + filters)
    whole = jnp.pad(maps[:, :, :quads], ((1, 1), (1, 1), (0, 0)))
    summed, taps = last_layer(
        shifted,
        grad_ext[1:-1, :, 1:-1],
        maps,
        whole,
        1.0 / math.sqrt(height2 * full2),
        3,
    )
    scale = 1.0 / math.sqrt(band * rows * width * strips)
    grad_one = summed.astype(jnp.float32).reshape(channels, 3, 3, channels) * scale
    grad_two = jnp.transpose(taps, (1, 0, 2)).reshape(filters, 3, 3, quads)

    input_grad = conv_valid(
        jnp.transpose(grad_ext, (1, 0, 2)), flip_kernel(filters_one), ("NCHW", "OHWI", "NCHW")
    ).astype(jnp.bfloat16)

    return (input_grad, grad_one, grad_two)


def solution(mesh):
    in_specs = (
        P("grp", "row", ("col", "pair")),
        P(),
        P("row", None, None, None),
        P(("grp", "row"), ("col", "pair"), None),
    )
    out_specs = (
        P("grp", "row", ("col", "pair")),
        P("grp", None, None, None),
        P(("grp", "row"), None, None, None),
    )
    return jax.shard_map(local, mesh=mesh, in_specs=in_specs, out_specs=out_specs, check_vma=False)
```

```python
import functools
import math

import jax
import jax.numpy as jnp
from jax import lax
from jax.experimental import pallas as pl
from jax.experimental.pallas import tpu as pltpu
from jax.sharding import PartitionSpec as P

MESH = pl.DeviceIdType.MESH
VMEM = pl.BlockSpec(memory_space=pltpu.VMEM)
STRIP = ("col", "pair")


def place():
    return lax.axis_index("row"), lax.axis_index(STRIP)


def device_at(row, strip):
    pairs = lax.axis_size("pair")
    return (lax.axis_index("grp"), row, lax.div(strip, pairs), lax.rem(strip, pairs))


def params(number):
    share = max(1, lax.axis_size("row") * lax.axis_size(STRIP) // 64)
    return pltpu.CompilerParams(
        collective_id=number, has_side_effects=True, vmem_limit_bytes=share * 24 * 1024 * 1024
    )


WAYS = [(a, b) for a in (-1, 0, 1) for b in (-1, 0, 1) if (a, b) != (0, 0)]


def first_kernel(
    rows, strips, cells, edge_up, kernel, pick_cols, spread_lanes,
    got_up, pre, gathered, shifted, near, block, send_sem, recv_sem, row_send, row_recv,
):
    row, strip = place()
    band, channels, width = cells.shape
    band2 = band // 4
    lanes = [pl.ds(0, width), pl.ds(width, width), pl.ds(2 * width, width)]
    tops = [pl.ds(0, 2), pl.ds(2, band), pl.ds(band + 2, 2)]

    def there(way):
        a, b = row + way[0], strip + way[1]
        return (a >= 0) & (a < rows) & (b >= 0) & (b < strips)

    barrier = pltpu.get_barrier_semaphore()
    for way in WAYS:
        if way[1] != 0:
            @pl.when(there(way))
            def _(way=way):
                pl.semaphore_signal(
                    barrier, inc=1, device_id=device_at(row + way[0], strip + way[1]), device_id_type=MESH
                )
    _, _, row_device = group("rows")
    for step in range(1, rows):
        pl.semaphore_signal(
            barrier, inc=1, device_id=row_device(lax.rem(row + step, rows)), device_id_type=MESH
        )

    def landing(way):
        return near.at[tops[way[0] + 1], :, lanes[way[1] + 1]]

    for way in WAYS:
        @pl.when(jnp.logical_not(there(way)))
        def _(way=way):
            slot = landing(way)
            slot[...] = jnp.zeros(slot.shape, slot.dtype)
            if way[0] == 0:
                slot = got_up.at[0 if way[1] < 0 else 1]
                slot[...] = jnp.zeros(slot.shape, slot.dtype)
    near[tops[1], :, lanes[1]] = cells[...]

    high = 1 + jnp.where(row > 0, 1, 0) + jnp.where(row < rows - 1, 1, 0)
    across = jnp.where(strip > 0, 1, 0) + jnp.where(strip < strips - 1, 1, 0)
    pl.semaphore_wait(barrier, high * across + rows - 1)

    def copy_to(way):
        back = (-way[0], -way[1])
        source = cells.at[[pl.ds(0, 2), pl.ds(0, band), pl.ds(band - 2, 2)][way[0] + 1]]
        return pltpu.make_async_remote_copy(
            src_ref=source,
            dst_ref=landing(back),
            send_sem=send_sem.at[WAYS.index(way)],
            recv_sem=recv_sem.at[WAYS.index(back)],
            device_id=device_at(row + way[0], strip + way[1]),
            device_id_type=MESH,
        )

    def upstream_to(way):
        side = 0 if way[1] < 0 else 1
        return pltpu.make_async_remote_copy(
            src_ref=edge_up.at[side],
            dst_ref=got_up.at[1 - side],
            send_sem=send_sem.at[8 + side],
            recv_sem=recv_sem.at[9 - side],
            device_id=device_at(row, strip + way[1]),
            device_id_type=MESH,
        )

    def arrival(way):
        back = (-way[0], -way[1])
        return pltpu.make_async_remote_copy(
            src_ref=landing(way),
            dst_ref=landing(way),
            send_sem=send_sem.at[WAYS.index(way)],
            recv_sem=recv_sem.at[WAYS.index(way)],
            device_id=device_at(row + back[0], strip + back[1]),
            device_id_type=MESH,
        )

    for way in sorted(WAYS, key=lambda w: (abs(w[0]), -abs(w[1]))):
        @pl.when(there(way))
        def _(way=way):
            copy_to(way).start()
    for way in ((0, -1), (0, 1)):
        @pl.when(there(way))
        def _(way=way):
            upstream_to(way).start()
    for way in WAYS:
        @pl.when(there(way))
        def _(way=way):
            arrival(way).wait_recv()

    full = 3 * width

    @pl.loop(0, band + 4)
    def _(h):
        here = near[h]
        wide = here.astype(jnp.float32)
        shifted[h, pl.ds(0, channels)] = pltpu.roll(wide, 1, 1).astype(jnp.bfloat16)
        shifted[h, pl.ds(channels, channels)] = here
        shifted[h, pl.ds(2 * channels, channels)] = pltpu.roll(wide, full - 1, 1).astype(jnp.bfloat16)

    @pl.loop(0, band + 2)
    def _(h):
        patches = shifted[pl.ds(h, 3)].reshape(9 * channels, full)
        pre[h] = jnp.dot(kernel[...], patches, preferred_element_type=jnp.float32)

    def silu(values):
        return values / (1.0 + jnp.exp(-values))

    contract = (((1,), (1,)), ((), ()))
    room = pick_cols.shape[0] // 2
    pooled = []
    for u in range(band2):
        total = jnp.zeros((room, 4 * channels), jnp.float32)
        for i in range(2):
            at = 1 + 4 * u + 2 * i
            pair_sum = (silu(pre[at]) + silu(pre[at + 1])) * 0.25
            upper = pair_sum.astype(jnp.bfloat16)
            lower = (pair_sum - upper.astype(jnp.float32)).astype(jnp.bfloat16)
            mean = lax.dot_general(pick_cols[...], upper, contract, preferred_element_type=jnp.float32)
            mean += lax.dot_general(pick_cols[...], lower, contract, preferred_element_type=jnp.float32)
            mean = mean.astype(jnp.bfloat16)
            for j in range(2):
                total += jnp.dot(
                    mean[j * room : (j + 1) * room],
                    spread_lanes[2 * i + j],
                    preferred_element_type=jnp.float32,
                )
        pooled.append(total)
    pooled = jnp.concatenate(pooled, 0).astype(jnp.bfloat16)
    block[...] = pooled
    finish = post(rows, row, row_device, lambda peer: block, gathered, row_send, row_recv)
    gathered[row] = pooled
    for way in WAYS:
        @pl.when(there(way))
        def _(way=way):
            copy_to(way).wait_send()
            if way[0] == 0:
                upstream_to(way).wait_send()
                upstream_to((-way[0], -way[1])).wait_recv()
    finish()


def first_layer(features_in, upstream, filters_one, number):
    channels, band, width = features_in.shape
    rows, strips = lax.axis_size("row"), lax.axis_size(STRIP)
    strip = lax.axis_index(STRIP)
    band2, width2 = band // 4, width // 4
    quads = 4 * channels
    near2 = width2 + 6
    room = -(-near2 // 16) * 16
    if (band2 * (-(-near2 // 8) * 8)) % 16 == 0:
        room = -(-near2 // 8) * 8
    height2, _, filters = upstream.shape
    cells = jnp.transpose(features_in, (1, 0, 2))
    edge_up = jnp.stack(
        [upstream[:, :2].reshape(2 * height2, filters), upstream[:, -2:].reshape(2 * height2, filters)]
    )
    v = jnp.arange(room)
    start = width + 4 * (v - 3)[None, :, None] + 2 * jnp.arange(2)[:, None, None]
    lane = jnp.arange(3 * width)[None, None, :]
    at_col = strip * width2 - 3 + v
    inside = (v < near2) & (at_col >= 0) & (at_col < width2 * strips)
    pick_cols = ((lane == start) | (lane == start + 1)) & inside[None, :, None]
    pick_cols = pick_cols.astype(jnp.bfloat16).reshape(2 * room, 3 * width)
    target = 4 * jnp.arange(channels)[None, :, None] + jnp.arange(4)[:, None, None]
    spread_lanes = (jnp.arange(quads)[None, None] == target).astype(jnp.bfloat16)
    got_up, pre, gathered, shifted = pl.pallas_call(
        functools.partial(first_kernel, rows, strips),
        out_shape=(
            jax.ShapeDtypeStruct(edge_up.shape, jnp.bfloat16),
            jax.ShapeDtypeStruct((band + 2, channels, 3 * width), jnp.float32),
            jax.ShapeDtypeStruct((rows, band2 * room, quads), jnp.bfloat16),
            jax.ShapeDtypeStruct((band + 4, 3 * channels, 3 * width), jnp.bfloat16),
        ),
        in_specs=[VMEM] * 5,
        out_specs=(VMEM,) * 4,
        scratch_shapes=[
            pltpu.VMEM((band + 4, channels, 3 * width), jnp.bfloat16),
            pltpu.VMEM((band2 * room, quads), jnp.bfloat16),
        ]
        + sems(10)
        + sems(rows),
        compiler_params=params(number),
    )(cells, edge_up, filters_one.reshape(channels, 9 * channels), pick_cols, spread_lanes)
    own = gathered.reshape(rows * band2, room, quads)[:, :near2]
    got_up = got_up.reshape(2, height2, 2, filters)
    inner = slice(width - 1, 2 * width + 1)
    return (
        shifted,
        pre[:, :, inner],
        own,
        jnp.concatenate([got_up[0], upstream, got_up[1]], 1),
    )


def post(count, me, device_of, source, landing, send_sem, recv_sem):
    def copy_of(step):
        peer = lax.rem(me + step, count)
        return pltpu.make_async_remote_copy(
            src_ref=source(peer),
            dst_ref=landing.at[me],
            send_sem=send_sem.at[step],
            recv_sem=recv_sem.at[me],
            device_id=device_of(peer),
            device_id_type=MESH,
        )

    def arrival(step):
        peer = lax.rem(me + step, count)
        return pltpu.make_async_remote_copy(
            src_ref=source(peer),
            dst_ref=landing.at[peer],
            send_sem=send_sem.at[step],
            recv_sem=recv_sem.at[peer],
            device_id=device_of(peer),
            device_id_type=MESH,
        )

    @pl.loop(1, count)
    def _(step):
        copy_of(step).start()

    def finish():
        @pl.loop(1, count)
        def _(step):
            copy_of(step).wait_send()
            arrival(step).wait_recv()

    return finish


def group(kind):
    rows, strips = lax.axis_size("row"), lax.axis_size(STRIP)
    row, strip = place()
    if kind == "all":
        return (
            rows * strips,
            row * strips + strip,
            lambda i: device_at(lax.div(i, strips), lax.rem(i, strips)),
        )
    if kind == "strips":
        return strips, strip, lambda i: device_at(row, i)
    return rows, row, lambda i: device_at(i, strip)


def sems(count):
    return [pltpu.SemaphoreType.DMA((count,)), pltpu.SemaphoreType.DMA((count,))]


def group_size(kind):
    rows, strips = lax.axis_size("row"), lax.axis_size(STRIP)
    return dict(all=rows * strips, strips=strips, rows=rows)[kind]


def total_of(count, landing):
    return lax.fori_loop(
        1,
        count,
        lambda i, value: value + landing[i].astype(jnp.float32),
        landing[0].astype(jnp.float32),
    )


def scatter_kernel(
    blocks, strip_map, out, maps, landing, send_sem, recv_sem, map_send, map_recv, on_send
):
    rows, me, row_device = group("rows")
    row, strip = place()
    cols, pairs = lax.axis_size("col"), lax.axis_size("pair")
    col, pair = lax.axis_index("col"), lax.axis_index("pair")

    barrier = pltpu.get_barrier_semaphore()
    for step in range(1, rows):
        pl.semaphore_signal(
            barrier, inc=1, device_id=row_device(lax.rem(me + step, rows)), device_id_type=MESH
        )
    for step in range(1, cols):
        pl.semaphore_signal(
            barrier,
            inc=1,
            device_id=device_at(row, lax.rem(col + step, cols) * pairs + pair),
            device_id_type=MESH,
        )
    for step in range(1, pairs):
        pl.semaphore_signal(
            barrier,
            inc=1,
            device_id=device_at(row, col * pairs + lax.rem(pair + step, pairs)),
            device_id_type=MESH,
        )
    pl.semaphore_wait(barrier, rows + cols + pairs - 3)

    def across(step):
        return pltpu.make_async_remote_copy(
            src_ref=strip_map,
            dst_ref=maps.at[strip],
            send_sem=map_send.at[step],
            recv_sem=map_recv.at[strip],
            device_id=device_at(row, lax.rem(col + step, cols) * pairs + pair),
            device_id_type=MESH,
        )

    def onward(source, column, step):
        slot = column * pairs + pair
        return pltpu.make_async_remote_copy(
            src_ref=source,
            dst_ref=maps.at[slot],
            send_sem=on_send.at[column * pairs + step],
            recv_sem=map_recv.at[slot],
            device_id=device_at(row, col * pairs + lax.rem(pair + step, pairs)),
            device_id_type=MESH,
        )

    def arrival(slot):
        return pltpu.make_async_remote_copy(
            src_ref=strip_map,
            dst_ref=maps.at[slot],
            send_sem=map_send.at[0],
            recv_sem=map_recv.at[slot],
            device_id=device_at(row, strip),
            device_id_type=MESH,
        )

    for step in range(1, cols):
        across(step).start()
    finish = post(rows, me, row_device, lambda peer: blocks.at[peer], landing, send_sem, recv_sem)
    for step in range(1, pairs):
        onward(strip_map, col, step).start()
    landing[me] = blocks[me]
    maps[strip] = strip_map[...]
    for step in range(1, cols):
        column = lax.rem(col + step, cols)
        slot = column * pairs + pair
        arrival(slot).wait_recv()
        for other in range(1, pairs):
            onward(maps.at[slot], column, other).start()
    finish()
    out[...] = total_of(rows, landing).astype(out.dtype)
    for step in range(1, cols):
        across(step).wait_send()
    for step in range(cols):
        column = lax.rem(col + step, cols)
        for other in range(1, pairs):
            onward(strip_map, column, other).wait_send()
            arrival(column * pairs + lax.rem(pair + other, pairs)).wait_recv()


def reduce_scatter(blocks, strip_map, number):
    rows, strips = group_size("rows"), group_size("strips")
    return pl.pallas_call(
        scatter_kernel,
        out_shape=(
            jax.ShapeDtypeStruct(blocks.shape[1:], jnp.bfloat16),
            jax.ShapeDtypeStruct((strips,) + strip_map.shape, strip_map.dtype),
        ),
        in_specs=[VMEM] * 2,
        out_specs=(VMEM,) * 2,
        scratch_shapes=[pltpu.VMEM(blocks.shape, blocks.dtype)]
        + sems(rows)
        + sems(strips)
        + [pltpu.SemaphoreType.DMA((strips,))],
        compiler_params=params(number),
    )(blocks, strip_map)


def last_kernel(
    scale, shifted, gradient, maps, whole, out, taps, turned, blocks, landing, part, parts, mine, *semaphores
):
    rows, row, row_device = group("rows")
    strips, strip, strip_device = group("strips")
    barrier = pltpu.get_barrier_semaphore()
    for step in range(1, rows):
        pl.semaphore_signal(
            barrier, inc=1, device_id=row_device(lax.rem(row + step, rows)), device_id_type=MESH
        )
    for step in range(1, strips):
        pl.semaphore_signal(
            barrier, inc=1, device_id=strip_device(lax.rem(strip + step, strips)), device_id_type=MESH
        )
    band, channels, width = gradient.shape
    steps, filters, spots = turned.shape
    full2 = whole.shape[1] - 2
    chunk = spots // full2
    quads = whole.shape[2]

    def one_row(h, total):
        patches = shifted[pl.ds(h + 1, 3), :, pl.ds(width, width)].reshape(9 * channels, width)
        return total + lax.dot_general(
            gradient[h], patches, (((1,), (1,)), ((), ())), preferred_element_type=jnp.float32
        )

    total = lax.fori_loop(0, band, one_row, jnp.zeros((channels, 9 * channels), jnp.float32))
    height = channels // strips
    for peer in range(strips):
        blocks[peer] = total[peer * height : (peer + 1) * height].astype(blocks.dtype)

    for step in range(steps):
        rows_of = maps[pl.ds(step * chunk, chunk), :, pl.ds(quads, filters)].reshape(spots, filters)
        turned[step] = rows_of.astype(jnp.float32).T.astype(turned.dtype)

    def tap(index):
        first, second = divmod(index, 3)

        def product(step):
            window = whole[pl.ds(step * chunk + first, chunk), pl.ds(second, full2)]
            return scale * jnp.dot(
                turned[step], window.reshape(spots, quads), preferred_element_type=jnp.float32
            )

        taps[index] = product(0)
        if steps > 1:
            @pl.loop(1, steps)
            def _(step):
                taps[index] += product(step)

    pl.semaphore_wait(barrier, rows + strips - 2)
    one, two, three = semaphores[:2], semaphores[2:4], semaphores[4:]
    finish = post(strips, strip, strip_device, lambda peer: blocks.at[peer], landing, *one)
    landing[strip] = blocks[strip]
    for index in range(3):
        tap(index)
    finish()
    total = total_of(strips, landing).astype(part.dtype)
    part[...] = total
    finish = post(rows, row, row_device, lambda peer: part, parts, *two)
    parts[row] = total
    for index in range(3, 6):
        tap(index)
    finish()
    total = total_of(rows, parts).astype(part.dtype)
    mine[...] = total
    finish = post(strips, strip, strip_device, lambda peer: mine, out, *three)
    out[strip] = total
    for index in range(6, 9):
        tap(index)
    finish()


def last_layer(shifted, gradient, maps, whole, scale, number):
    rows, strips = group_size("rows"), group_size("strips")
    channels = gradient.shape[1]
    kind = jnp.bfloat16
    height2, full2, depth = maps.shape
    filters = depth - whole.shape[2]
    chunk = max(1, 1024 // full2)
    piece = (channels // strips, 9 * channels)
    return pl.pallas_call(
        functools.partial(last_kernel, scale),
        out_shape=(
            jax.ShapeDtypeStruct((strips,) + piece, kind),
            jax.ShapeDtypeStruct((9, filters, whole.shape[2]), jnp.float32),
        ),
        in_specs=[VMEM] * 4,
        out_specs=(VMEM,) * 2,
        scratch_shapes=[
            pltpu.VMEM((height2 // chunk, filters, chunk * full2), kind),
            pltpu.VMEM((strips,) + piece, kind),
            pltpu.VMEM((strips,) + piece, kind),
            pltpu.VMEM(piece, kind),
            pltpu.VMEM((rows,) + piece, kind),
            pltpu.VMEM(piece, kind),
        ]
        + sems(strips)
        + sems(rows)
        + sems(strips),
        compiler_params=params(number),
    )(shifted, gradient, maps, whole)


def conv_valid(cells, kernel, numbers):
    return lax.conv_general_dilated(
        cells[None], kernel, (1, 1), "VALID", dimension_numbers=numbers, preferred_element_type=jnp.float32
    )[0]


def flip_kernel(kernel):
    return jnp.transpose(kernel[:, ::-1, ::-1, :], (3, 1, 2, 0))


def silu_slope(values):
    sigmoid_value = jax.nn.sigmoid(values)
    return sigmoid_value * (1.0 + values * (1.0 - sigmoid_value))


def local(features_in, filters_one, filters_two, out_grad):
    channels, band, width = features_in.shape
    rows, strips = lax.axis_size("row"), lax.axis_size(STRIP)
    row, strip = place()
    quads = channels * 4
    band2, width2 = band // 4, width // 4
    height2, full2 = band2 * rows, width2 * strips
    filters = filters_two.shape[0]

    shifted, pre_one, own, upstream = first_layer(
        features_in, jnp.transpose(out_grad, (2, 1, 0)), filters_one, 0
    )
    pre_two = conv_valid(
        jnp.pad(own, ((1, 1), (0, 0), (0, 0))), filters_two, ("NHWC", "OHWI", "NHWC")
    )
    near = (upstream.astype(jnp.float32) * silu_slope(pre_two)).astype(jnp.bfloat16)

    spread = conv_valid(
        jnp.pad(near, ((1, 1), (0, 0), (0, 0))), flip_kernel(filters_two), ("NHWC", "OHWI", "NHWC")
    )
    channel = jnp.arange(quads)
    low_row = (channel // 2) % 2 == 1
    low_col = channel % 2 == 1
    tall = jnp.pad(spread, ((1, 1), (0, 0), (0, 0)))
    bands = spread.reshape(rows, band2, width2 + 2, quads)
    rim = jnp.where(low_row, tall[0:height2:band2], tall[band2 + 1 : height2 + 2 : band2])
    bands = jnp.concatenate([bands, rim[:, None]], 1)
    edge = jnp.where(low_col, bands[:, :, :1], bands[:, :, -1:])
    bands = jnp.concatenate([bands[:, :, 1:-1], edge], 2).astype(jnp.bfloat16)
    spots = (band2 + 1) * (width2 + 1)
    bands = jnp.pad(bands.reshape(rows, spots, quads), ((0, 0), (0, -spots % 16), (0, 0)))
    strip_map = jnp.concatenate([own[:, 3:-3], near[:, 2:-2]], 2).reshape(height2 * width2, quads + filters)
    grad_pooled, maps = reduce_scatter(bands, strip_map, 2)

    by_part = jnp.arange(quads)
    order = 4 * (by_part % channels) + by_part // channels
    pick = (channel[:, None] == order[None]).astype(jnp.bfloat16)
    parts = jnp.dot(grad_pooled[:spots], pick, preferred_element_type=jnp.float32).astype(jnp.bfloat16)
    parts = parts.reshape(band2 + 1, width2 + 1, 2, 2, channels)
    source = (jnp.arange(width + 2) + 1) // 2
    source = jnp.where(source == 0, 2 * width2 + 1, source - 1)
    place_of = 2 * jnp.arange(width2 + 1)[:, None] + jnp.arange(2)[None]
    expand = (place_of[:, :, None] == source[None, None]).astype(jnp.bfloat16)
    halves = jnp.einsum("uvijc,vjw->uicw", parts, expand, preferred_element_type=jnp.float32)
    halves = halves.reshape(2 * band2 + 2, channels, width + 2)
    halves = jnp.concatenate([halves[-1:], halves[:-1]], 0)
    tall_grad = jnp.repeat(halves, 2, 0)[1:-1] * 0.25
    at_row = row * band - 1 + jnp.arange(band + 2)
    at_col = strip * width - 1 + jnp.arange(width + 2)
    inside = ((at_row >= 0) & (at_row < band * rows))[:, None, None] & (
        (at_col >= 0) & (at_col < width * strips)
    )
    grad_ext = jnp.where(inside, tall_grad * silu_slope(pre_one), 0.0).astype(jnp.bfloat16)

    maps = jnp.transpose(maps.reshape(strips, height2, width2, quads + filters), (1, 0, 2, 3))
    maps = maps.reshape(height2, full2, quads + filters)
    whole = jnp.pad(maps[:, :, :quads], ((1, 1), (1, 1), (0, 0)))
    summed, taps = last_layer(
        shifted,
        grad_ext[1:-1, :, 1:-1],
        maps,
        whole,
        1.0 / math.sqrt(height2 * full2),
        3,
    )
    grad_ext, summed = lax.optimization_barrier((grad_ext, summed))
    scale = 1.0 / math.sqrt(band * rows * width * strips)
    grad_one = summed.astype(jnp.float32).reshape(channels, 3, 3, channels) * scale
    grad_two = jnp.transpose(taps, (1, 0, 2)).reshape(filters, 3, 3, quads)

    input_grad = conv_valid(
        jnp.transpose(grad_ext, (1, 0, 2)), flip_kernel(filters_one), ("NCHW", "OHWI", "NCHW")
    ).astype(jnp.bfloat16)

    return (input_grad, grad_one, grad_two)


def solution(mesh):
    in_specs = (
        P("grp", "row", ("col", "pair")),
        P(),
        P("row", None, None, None),
        P(("grp", "row"), ("col", "pair"), None),
    )
    out_specs = (
        P("grp", "row", ("col", "pair")),
        P("grp", None, None, None),
        P(("grp", "row"), None, None, None),
    )
    return jax.shard_map(local, mesh=mesh, in_specs=in_specs, out_specs=out_specs, check_vma=False)
```
